32 devices in a mesh: groups: 2 (over y), ctx: 8 (over z, x), tp: 2 (over core).
Axes of the slice: x: 2, y: 2, z: 4, core: 2. Of those that a mesh axis runs over, the one named last changes fastest.
Arguments:
- queries: bfloat16 [2048, 4096], P(('groups', 'ctx'), 'tp'), parts along dimension 0, may hold values from -6 to 6
- keys: bfloat16 [2048, 4096], P(('groups', 'ctx'), 'tp'), parts along dimension 0, may hold values from -6 to 6
- values: bfloat16 [2048, 4096], P(('groups', 'ctx'), 'tp'), parts along dimension 0, may hold values from -30 to 30
- grad_y: bfloat16 [2048, 4096], P(('groups', 'ctx'), 'tp'), parts along dimension 0, may hold values from -6 to 6
- state_low: bfloat16 [16, 32, 128, 128], P(('groups', 'ctx'), 'tp'), parts along dimension 0, may hold values from -48 to 48
- gain: float32 [4096], P('tp'), may hold values from 0.5 to 2
Outputs:
- grad_query: bfloat16 [2048, 4096], P(('groups', 'ctx'), 'tp'), parts along dimension 0
- grad_key: bfloat16 [2048, 4096], P(('groups', 'ctx'), 'tp'), parts along dimension 0
- grad_value: bfloat16 [2048, 4096], P(('groups', 'ctx'), 'tp'), parts along dimension 0
The draws below stay inside these ranges and needn't reach their ends.
There are 2 independent parts, one for each index of `groups`. The reference program is written for one: setup_inputs(seed, part) draws one part's arguments, and reference() takes and returns one part's arrays. A program takes and returns all parts, laid end to end along the dimension named above; an argument that names none is the same for every part. Nothing has to cross between parts.
All inputs are finite; a program needn't handle non-finite values.
Results may differ from the reference program's by a relative error of at most 0.0058.
Values sent between devices are 32-bit elements; how exact they have to be, the bound alone decides.
No kernel may reach another device: no remote copies, remote signals or barrier semaphores. Data moves between devices by JAX's collectives and lax.ppermute only.
A program may use at most 64 MiB of HBM per device.

```python
import math
import jax
import jax.numpy as jnp
from jax import lax

HEADS = 32
HEAD = 128
TOK_DEV = 128
TOKENS = 1024
BLOCKS = 8
FEATURES = 4096


def draw_values(key, part):
    key = jax.random.fold_in(key, 7)
    base_key, scale_key = jax.random.split(key, 2)
    column_scale = jnp.exp(jax.random.uniform(scale_key, (FEATURES,), jnp.float32, math.log(0.5), math.log(5.0)))
    base = jnp.clip(jax.random.normal(base_key, (TOKENS, FEATURES), jnp.float32), -6.0, 6.0)
    return (base * column_scale).astype(jnp.bfloat16)


def block_scale(key, shape, shards, low, top_value):
    level = 1.0
    for axis_at, blocks in shards:
        draws = jax.random.uniform(jax.random.fold_in(jax.random.fold_in(key, 6), axis_at), (blocks,), jnp.float32, low / len(shards), top_value / len(shards))
        level = level * jnp.repeat(jnp.exp(draws), shape[axis_at] // blocks).reshape((-1,) + (1,) * (len(shape) - 1 - axis_at))
    return level


def noise(own_key, shape, scale, bound, shards=(), dtype=jnp.bfloat16):
    values = scale * jax.random.normal(own_key, shape, jnp.float32)
    if shards:
        values = values * block_scale(own_key, shape, shards, -0.22, 0.18)
    return jnp.clip(values, -bound, bound).astype(dtype)


def setup_inputs(seed: int = 0, part: int = 0) -> dict:
    key_of = jax.random.split(jax.random.key(seed), 7)
    own_keys = jax.random.split(jax.random.fold_in(key_of[6], part), 7)
    return {
        "queries": noise(own_keys[0], (TOKENS, FEATURES), 1.0, 6.0, ((0, 8), (1, 2))),
        "keys": noise(own_keys[1], (TOKENS, FEATURES), 1.0, 6.0, ((0, 8), (1, 2))),
        "values": draw_values(jax.random.fold_in(jax.random.fold_in(key_of[6], part), 71), part),
        "grad_y": noise(own_keys[3], (TOKENS, FEATURES), 1.0, 6.0, ((0, 8), (1, 2))),
        "state_low": noise(own_keys[4], (BLOCKS, HEADS, HEAD, HEAD), 8.0, 48.0, ((0, 8), (1, 2))),
        "gain": jnp.clip(jnp.exp(math.log(2.0) - 1.3862944 * jax.random.uniform(key_of[5], (FEATURES,), jnp.float32) ** block_scale(key_of[5], (FEATURES,), ((0, 2),), -0.2, 0.2)), 0.5, 2.0),
    }


def reference(queries, keys, values, grad_y, state_low, gain):
    blocks = TOKENS // TOK_DEV
    block_shape = (blocks, TOK_DEV, HEADS, HEAD)
    query_rows = queries.reshape(block_shape)
    key_rows = keys.reshape(block_shape)
    value_rows = values.reshape(block_shape)
    grad_rows = grad_y.reshape(block_shape)
    gain_rows = gain.reshape(HEADS, HEAD).astype(jnp.float32)
    lower_mask = (lax.broadcasted_iota(jnp.int32, (TOK_DEV, TOK_DEV), 0) >= lax.broadcasted_iota(jnp.int32, (TOK_DEV, TOK_DEV), 1)).astype(jnp.float32)
    empty_state = jnp.zeros((HEADS, HEAD, HEAD), jnp.float32)

    def forward(pieces):
        query_now, key_now, value_now, grad_now, state_now = pieces
        query_full = query_now.astype(jnp.float32)
        key_full = key_now.astype(jnp.float32)
        value_full = value_now.astype(jnp.float32)
        scores = jnp.einsum('tha,sha->hts', query_full, key_full)
        probs = (scores * lower_mask).astype(jnp.bfloat16)
        attn_out = jnp.einsum('hts,shb->thb', probs.astype(jnp.float32), value_full)
        attn_out = attn_out + jnp.einsum('tha,hab->thb', query_full, state_now.astype(jnp.float32))
        weighted = gain_rows * grad_now.astype(jnp.float32)
        square_sum = lax.optimization_barrier(jnp.sum(attn_out * attn_out, axis=(1, 2)))
        cross_sum = lax.optimization_barrier(jnp.sum(weighted * attn_out, axis=(1, 2)))
        inv_rms = 1.0 / jnp.sqrt(square_sum / FEATURES + 1e-06)
        grad_out = inv_rms[:, None, None] * weighted - attn_out * (cross_sum * inv_rms ** 3 / FEATURES)[:, None, None]
        return (probs, grad_out.astype(jnp.bfloat16))
    probs_all, grad_outs = lax.map(forward, (query_rows, key_rows, value_rows, grad_rows, state_low))

    def backward(later_sum, pieces):
        query_now, key_now, value_now, state_now, probs, grad_out = pieces
        query_full = query_now.astype(jnp.float32)
        key_full = key_now.astype(jnp.float32)
        value_full = value_now.astype(jnp.float32)
        grad_full = grad_out.astype(jnp.float32)
        grad_low = later_sum.astype(jnp.bfloat16).astype(jnp.float32)
        grad_probs = (jnp.einsum('thb,shb->hts', grad_full, value_full) * lower_mask).astype(jnp.bfloat16).astype(jnp.float32)
        grad_query = jnp.einsum('hts,sha->tha', grad_probs, key_full) + jnp.einsum('thb,hab->tha', grad_full, state_now.astype(jnp.float32))
        grad_key = jnp.einsum('hts,tha->sha', grad_probs, query_full) + jnp.einsum('shb,hab->sha', value_full, grad_low)
        grad_value = jnp.einsum('hts,thb->shb', probs.astype(jnp.float32), grad_full) + jnp.einsum('sha,hab->shb', key_full, grad_low)
        updated = later_sum + jnp.einsum('tha,thb->hab', query_full, grad_full)
        return (updated, (grad_query.astype(jnp.bfloat16), grad_key.astype(jnp.bfloat16), grad_value.astype(jnp.bfloat16)))
    _, (grad_query, grad_key, grad_value) = lax.scan(backward, empty_state, (query_rows, key_rows, value_rows, state_low, probs_all, grad_outs), reverse=True)
    flat = (TOKENS, FEATURES)
    return (grad_query.reshape(flat), grad_key.reshape(flat), grad_value.reshape(flat))
```

```python
import functools

import jax
import jax.numpy as jnp
from jax import lax
from jax.experimental import pallas as pl
from jax.experimental.pallas import tpu as pltpu
from jax.sharding import PartitionSpec as P

HEAD = 128
QUAD = 4
CHUNKS = 1
VMEM = pl.BlockSpec(memory_space=pltpu.VMEM)
NN = (((1,), (0,)), ((), ()))
NT = (((1,), (1,)), ((), ()))
TN = (((0,), (0,)), ((), ()))


def dot(left, right, dims):
    return lax.dot_general(left, right, dims, preferred_element_type=jnp.float32)


def columns(head):
    if isinstance(head, int):
        return pl.ds(head * HEAD, HEAD)
    return pl.ds(pl.multiple_of(head * HEAD, HEAD), HEAD)


def lower(rows):
    row = lax.broadcasted_iota(jnp.int32, (rows, rows), 0)
    return row >= lax.broadcasted_iota(jnp.int32, (rows, rows), 1)


def forward_kernel(q_ref, k_ref, v_ref, s_ref, y_ref, gain_ref, out_ref, probs_ref, stat_ref):
    rows = q_ref.shape[0]
    mask = lower(rows)
    squares = jnp.zeros((rows, HEAD), jnp.float32)
    crosses = jnp.zeros((rows, HEAD), jnp.float32)
    for head in range(q_ref.shape[1] // HEAD):
        at = columns(head)
        q = q_ref[:, at]
        probs = jnp.where(mask, dot(q, k_ref[:, at], NT), 0.0).astype(jnp.bfloat16)
        probs_ref[:, at] = probs
        out = dot(probs, v_ref[:, at], NN) + dot(q, s_ref[head], NN)
        out_ref[:, at] = out
        squares += out * out
        crosses += gain_ref[:, at] * y_ref[:, at].astype(jnp.float32) * out
    lane = lax.broadcasted_iota(jnp.int32, (rows, HEAD), 1)
    square = jnp.sum(squares, axis=1, keepdims=True)
    cross = jnp.sum(crosses, axis=1, keepdims=True)
    stat_ref[...] = jnp.where(lane == 0, square, cross)


def state_kernel(
    features, chunks, where_ref, own_ref, other_ref, out_ref, y_ref, gain_ref, q_ref, g_ref, *u_refs
):
    stat = own_ref[...] + other_ref[...]
    square, cross = stat[:, 0:1], stat[:, 1:2]
    inverse = lax.rsqrt(square / features + 1e-06)
    back = cross * (inverse * inverse * inverse) / features
    me = where_ref[0]
    heads = q_ref.shape[1] // HEAD
    share = heads // (QUAD * chunks)
    for chunk in range(chunks):
        for step in (3, 1, 2, 0):
            u_ref = u_refs[chunk * QUAD + step]
            for local in range(share):
                at = columns((chunk * QUAD + (me ^ step)) * share + local)
                weighted = gain_ref[:, at] * y_ref[:, at].astype(jnp.float32)
                grad = (inverse * weighted - out_ref[:, at] * back).astype(jnp.bfloat16)
                g_ref[:, at] = grad
                u_ref[local] = dot(q_ref[:, at], grad, TN)


def local_kernel(
    q_ref, k_ref, v_ref, s_ref, g_ref, probs_ref, query_ref, key_ref, value_ref
):
    mask = lower(q_ref.shape[0])
    for head in range(q_ref.shape[1] // HEAD):
        at = columns(head)
        g = g_ref[:, at]
        grads = jnp.where(mask, dot(g, v_ref[:, at], NT), 0.0).astype(jnp.bfloat16)
        query = dot(grads, k_ref[:, at], NN) + dot(g, s_ref[head], NT)
        query_ref[:, at] = query.astype(jnp.bfloat16)
        key_ref[:, at] = dot(grads, q_ref[:, at], TN)
        value_ref[:, at] = dot(probs_ref[:, at], g, TN)


def final_kernel(chunks, where_ref, k_ref, v_ref, key_in, value_in, *refs):
    later_refs, (key_ref, value_ref) = refs[:-2], refs[-2:]
    me = where_ref[0]
    heads = k_ref.shape[1] // HEAD
    share = heads // (QUAD * chunks)
    for chunk in range(chunks):
        for step in range(QUAD):
            for local in range(share):
                at = columns((chunk * QUAD + (me ^ step)) * share + local)
                later = later_refs[chunk * QUAD + step][local].astype(jnp.bfloat16)
                key = key_in[:, at] + dot(v_ref[:, at], later, NT)
                key_ref[:, at] = key.astype(jnp.bfloat16)
                value = value_in[:, at] + dot(k_ref[:, at], later, NN)
                value_ref[:, at] = value.astype(jnp.bfloat16)


def params(mib):
    return pltpu.CompilerParams(vmem_limit_bytes=mib << 20)


def partner(value, axis, mask):
    count = lax.axis_size(axis)
    return lax.ppermute(value, axis, [(source, source ^ mask) for source in range(count)])


def per_device(queries, keys, values, grad_y, state_low, gain):
    rows, width = queries.shape
    heads = width // HEAD
    chunks = CHUNKS
    share = heads // (QUAD * chunks)
    features = width * lax.axis_size("tp")
    state = state_low[0]
    gain_row = gain.reshape(1, width)
    place = lax.axis_index("ctx")
    me = place % QUAD
    where = me.reshape(1).astype(jnp.int32)
    smem = pl.BlockSpec(memory_space=pltpu.SMEM)

    full = jax.ShapeDtypeStruct((rows, width), jnp.float32)
    half = jax.ShapeDtypeStruct((rows, width), jnp.bfloat16)
    piece = jax.ShapeDtypeStruct((share, HEAD, HEAD), jnp.float32)
    out, probs, stat = pl.pallas_call(
        forward_kernel,
        out_shape=(full, half, jax.ShapeDtypeStruct((rows, HEAD), jnp.float32)),
        in_specs=[VMEM] * 6,
        out_specs=(VMEM,) * 3,
        compiler_params=params(20),
    )(queries, keys, values, state, grad_y, gain_row)
    other = partner(stat, "tp", 1)
    grad, *own = pl.pallas_call(
        functools.partial(state_kernel, features, chunks),
        out_shape=(half,) + (piece,) * (QUAD * chunks),
        in_specs=[smem] + [VMEM] * 6,
        out_specs=(VMEM,) * (1 + QUAD * chunks),
        compiler_params=params(20),
    )(where, stat, other, out, grad_y, gain_row, queries)

    held = []
    for chunk in range(chunks):
        mine = own[chunk * QUAD : (chunk + 1) * QUAD]
        held.append([mine[0]] + [partner(mine[step], "ctx", step) for step in (1, 2, 3)])
    later = []
    for chunk in range(chunks):
        total = held[chunk][0] + held[chunk][1] + held[chunk][2] + held[chunk][3]
        behind = jnp.zeros_like(total)
        span = QUAD
        while span < lax.axis_size("ctx"):
            came = partner(total, "ctx", span)
            behind = jnp.where((place & span) == 0, behind + came, behind)
            span *= 2
            if span < lax.axis_size("ctx"):
                total = total + came
        sums = []
        for target in range(QUAD):
            value = behind
            for source in range(QUAD):
                if source != target:
                    value = value + jnp.where((me ^ source) > (me ^ target), held[chunk][source], 0.0)
            sums.append(value)
        later += [sums[0]] + [partner(sums[step], "ctx", step) for step in (1, 2, 3)]

    grad_query, key_part, value_part = pl.pallas_call(
        local_kernel,
        out_shape=(half, full, full),
        in_specs=[VMEM] * 6,
        out_specs=(VMEM,) * 3,
        compiler_params=params(20),
    )(queries, keys, values, state, grad, probs)
    grad_key, grad_value = pl.pallas_call(
        functools.partial(final_kernel, chunks),
        out_shape=(half, half),
        in_specs=[smem] + [VMEM] * (4 + QUAD * chunks),
        out_specs=(VMEM,) * 2,
        compiler_params=params(20),
    )(where, keys, values, key_part, value_part, *later)
    return grad_query, grad_key, grad_value


def solution(mesh):
    rows = P(("groups", "ctx"), "tp")
    return jax.shard_map(
        per_device,
        mesh=mesh,
        in_specs=(rows, rows, rows, rows, P(("groups", "ctx"), "tp", None, None), P("tp")),
        out_specs=(rows, rows, rows),
        check_vma=False,
    )
```

```python
import functools

import jax
import jax.numpy as jnp
from jax import lax
from jax.experimental import pallas as pl
from jax.experimental.pallas import tpu as pltpu
from jax.sharding import PartitionSpec as P

HEAD = 128
QUAD = 4
SPLIT = (2, 2)
STEPS = (3, 1, 2, 0)
GROUPS = 4
VMEM = pl.BlockSpec(memory_space=pltpu.VMEM)
ANY = pl.BlockSpec(memory_space=pl.ANY)
HBM = pl.BlockSpec(memory_space=pltpu.HBM)
NN = (((1,), (0,)), ((), ()))
NT = (((1,), (1,)), ((), ()))
TN = (((0,), (0,)), ((), ()))


def dot(left, right, dims):
    return lax.dot_general(left, right, dims, preferred_element_type=jnp.float32)


def columns(head, count=1):
    if isinstance(head, int):
        return pl.ds(head * HEAD, count * HEAD)
    return pl.ds(pl.multiple_of(head * HEAD, HEAD), count * HEAD)


def lower(rows):
    row = lax.broadcasted_iota(jnp.int32, (rows, rows), 0)
    return row >= lax.broadcasted_iota(jnp.int32, (rows, rows), 1)


def parts_of(heads):
    each = heads // QUAD
    parts, start = [], 0
    for index, count in enumerate(SPLIT):
        count = each - start if index == len(SPLIT) - 1 else count
        parts.append((start, count))
        start += count
    return each, parts


def forward_kernel(
    q_hbm, k_hbm, v_hbm, s_hbm, y_hbm, gain_hbm,
    out_ref, probs_ref, stat_ref, q_ref, k_ref, v_ref, s_ref, y_ref, gain_ref, sems, gain_sem,
):
    rows, width = q_ref.shape
    heads = width // HEAD
    count = heads // GROUPS
    gain_copy = pltpu.make_async_copy(gain_hbm, gain_ref, gain_sem)
    copies = []
    for group in range(GROUPS):
        at = columns(group * count, count)
        span = pl.ds(group * count, count)
        pairs = [(q_hbm.at[:, at], q_ref.at[:, at]), (k_hbm.at[:, at], k_ref.at[:, at])]
        pairs += [(v_hbm.at[:, at], v_ref.at[:, at]), (s_hbm.at[span], s_ref.at[span])]
        pairs += [(y_hbm.at[:, at], y_ref.at[:, at])]
        copies.append(
            [
                pltpu.make_async_copy(source, target, sems.at[group, index])
                for index, (source, target) in enumerate(pairs)
            ]
        )
    for copy in copies[0] + [gain_copy] + sum(copies[1:], []):
        copy.start()
    mask = lower(rows)
    squares = jnp.zeros((rows, HEAD), jnp.float32)
    crosses = jnp.zeros((rows, HEAD), jnp.float32)
    for group in range(GROUPS):
        for copy in copies[group]:
            copy.wait()
        if group == 0:
            gain_copy.wait()
        for head in range(group * count, (group + 1) * count):
            at = columns(head)
            q = q_ref[:, at]
            probs = jnp.where(mask, dot(q, k_ref[:, at], NT), 0.0).astype(jnp.bfloat16)
            probs_ref[:, at] = probs
            out = dot(probs, v_ref[:, at], NN) + dot(q, s_ref[head], NN)
            out_ref[:, at] = out
            squares += out * out
            crosses += gain_ref[:, at] * y_ref[:, at].astype(jnp.float32) * out
    lane = lax.broadcasted_iota(jnp.int32, (rows, HEAD), 1)
    square = jnp.sum(squares, axis=1, keepdims=True)
    cross = jnp.sum(crosses, axis=1, keepdims=True)
    stat_ref[...] = jnp.where(lane == 0, square, cross)


def state_kernel(
    features, each, start, count, own_ref, other_ref, out_ref, y_ref, gain_ref, q_ref, *refs
):
    g_ref, *u_refs = refs[-1 - QUAD :]
    stat = own_ref[...] + other_ref[...]
    square, cross = stat[:, 0:1], stat[:, 1:2]
    inverse = lax.rsqrt(square / features + 1e-06)
    back = cross * (inverse * inverse * inverse) / features
    me = lax.rem(lax.axis_index("ctx"), QUAD)
    for step in STEPS:
        for local in range(count):
            at = columns((me ^ step) * each + start + local)
            weighted = gain_ref[:, at] * y_ref[:, at].astype(jnp.float32)
            grad = (inverse * weighted - out_ref[:, at] * back).astype(jnp.bfloat16)
            g_ref[:, columns(step * count + local)] = grad
            u_refs[step][local] = dot(q_ref[:, at], grad, TN)


def suffix_kernel(*refs):
    block_refs, behind_refs, sum_refs = refs[:QUAD], refs[QUAD:-QUAD], refs[-QUAD:]
    place = lax.axis_index("ctx")
    me = lax.rem(place, QUAD)
    blocks = [ref[...] for ref in block_refs]
    behind = jnp.zeros_like(blocks[0])
    for level, ref in enumerate(behind_refs):
        behind += jnp.where((place & (QUAD << level)) == 0, ref[...], 0.0)
    for target in STEPS:
        value = behind
        for source in range(QUAD):
            if source != target:
                value += jnp.where((me ^ source) > (me ^ target), blocks[source], 0.0)
        sum_refs[target][...] = value


def local_kernel(each, parts, q_ref, k_ref, v_ref, s_ref, probs_ref, *refs):
    g_refs, query_ref = refs[: len(parts)], refs[len(parts)]
    key_refs = refs[len(parts) + 1 : 2 * len(parts) + 1]
    value_refs = refs[2 * len(parts) + 1 :]
    mask = lower(q_ref.shape[0])
    me = lax.rem(lax.axis_index("ctx"), QUAD)
    for part, (start, count) in enumerate(parts):
        for step in range(QUAD):
            for local in range(count):
                head = (me ^ step) * each + start + local
                at, slot = columns(head), columns(step * count + local)
                g = g_refs[part][:, slot]
                grads = jnp.where(mask, dot(g, v_ref[:, at], NT), 0.0).astype(jnp.bfloat16)
                query = dot(grads, k_ref[:, at], NN) + dot(g, s_ref[head], NT)
                query_ref[:, at] = query.astype(jnp.bfloat16)
                key_refs[part][:, slot] = dot(grads, q_ref[:, at], TN)
                value_refs[part][:, slot] = dot(probs_ref[:, at], g, TN)


def final_kernel(each, start, count, k_ref, v_ref, key_in, value_in, *refs):
    later_refs = refs[:QUAD]
    key_hbm, value_hbm, key_ref, value_ref, sems = refs[-5:]
    me = lax.rem(lax.axis_index("ctx"), QUAD)
    copies = []
    for step in (0, 1, 2, 3):
        slots = columns(step * count, count)
        for local in range(count):
            at = columns((me ^ step) * each + start + local)
            slot = columns(step * count + local)
            later = later_refs[step][local].astype(jnp.bfloat16)
            key = key_in[:, slot] + dot(v_ref[:, at], later, NT)
            key_ref[:, slot] = key.astype(jnp.bfloat16)
            value = value_in[:, slot] + dot(k_ref[:, at], later, NN)
            value_ref[:, slot] = value.astype(jnp.bfloat16)
        at = columns((me ^ step) * each + start, count)
        for index, (source, target) in enumerate(((key_ref, key_hbm), (value_ref, value_hbm))):
            copy = pltpu.make_async_copy(source.at[:, slots], target.at[:, at], sems.at[step, index])
            copy.start()
            copies.append(copy)
    for copy in copies:
        copy.wait()


def params(mib):
    return pltpu.CompilerParams(vmem_limit_bytes=mib << 20)


def partner(value, axis, mask):
    count = lax.axis_size(axis)
    return lax.ppermute(value, axis, [(source, source ^ mask) for source in range(count)])


def per_device(queries, keys, values, grad_y, state_low, gain):
    rows, width = queries.shape
    heads = width // HEAD
    each, parts = parts_of(heads)
    features = width * lax.axis_size("tp")
    state = state_low[0]
    gain_row = gain.reshape(1, width)

    near = pltpu.VMEM
    half = jax.ShapeDtypeStruct((rows, width), jnp.bfloat16)
    held_half = near((rows, width), jnp.bfloat16)
    operands = (queries, keys, values, state, grad_y, gain_row)
    out, probs, stat, q, k, v, s, y, gain_v = pl.pallas_call(
        forward_kernel,
        out_shape=(
            near((rows, width), jnp.float32),
            held_half,
            near((rows, HEAD), jnp.float32),
            held_half,
            held_half,
            held_half,
            near(state.shape, state.dtype),
            held_half,
            near(gain_row.shape, gain_row.dtype),
        ),
        in_specs=[HBM] * 6,
        out_specs=(VMEM,) * 9,
        scratch_shapes=[pltpu.SemaphoreType.DMA((GROUPS, 5)), pltpu.SemaphoreType.DMA],
        compiler_params=params(8),
    )(*(pltpu.with_memory_space_constraint(value, pltpu.HBM) for value in operands))
    other = partner(stat, "tp", 1)

    grads, held = [], []
    for start, count in parts:
        tokens = held[-1][1:2] if held else []
        piece = near((count, HEAD, HEAD), jnp.float32)
        grad, *own = pl.pallas_call(
            functools.partial(state_kernel, features, each, start, count),
            out_shape=(near((rows, QUAD * count * HEAD), jnp.bfloat16),) + (piece,) * QUAD,
            in_specs=[VMEM] * 6 + [ANY] * len(tokens),
            out_specs=(VMEM,) * (1 + QUAD),
            compiler_params=params(8),
        )(stat, other, out, y, gain_v, q, *tokens)
        grads.append(grad)
        came = {step: partner(own[step], "ctx", step) for step in (3, 1, 2)}
        held.append([own[0], came[1], came[2], came[3]])
    later = []
    for blocks in held:
        total = blocks[0] + blocks[1] + blocks[2] + blocks[3]
        behind = []
        span = QUAD
        while span < lax.axis_size("ctx"):
            behind.append(partner(total, "ctx", span))
            span *= 2
            if span < lax.axis_size("ctx"):
                total = total + behind[-1]
        piece = near(total.shape, jnp.float32)
        sums = pl.pallas_call(
            suffix_kernel,
            out_shape=(piece,) * QUAD,
            in_specs=[VMEM] * (QUAD + len(behind)),
            out_specs=(VMEM,) * QUAD,
            compiler_params=params(8),
        )(*blocks, *behind)
        came = {step: partner(sums[step], "ctx", step) for step in (3, 1, 2)}
        later.append([sums[0], came[1], came[2], came[3]])

    slots = [near((rows, QUAD * count * HEAD), jnp.float32) for _, count in parts]
    grad_query, *local = pl.pallas_call(
        functools.partial(local_kernel, each, parts),
        out_shape=(half, *slots, *slots),
        in_specs=[VMEM] * (5 + len(parts)),
        out_specs=(VMEM,) * (1 + 2 * len(parts)),
        compiler_params=params(8),
    )(q, k, v, s, probs, *grads)
    done = ()
    for part, (start, count) in enumerate(parts):
        stage = pltpu.VMEM((rows, QUAD * count * HEAD), jnp.bfloat16)
        done = pl.pallas_call(
            functools.partial(final_kernel, each, start, count),
            out_shape=(half, half),
            in_specs=[VMEM] * (4 + QUAD) + [HBM] * len(done),
            out_specs=(HBM,) * 2,
            scratch_shapes=[stage, stage, pltpu.SemaphoreType.DMA((QUAD, 2))],
            input_output_aliases={4 + QUAD + index: index for index in range(len(done))},
            compiler_params=params(8),
        )(k, v, local[part], local[len(parts) + part], *later[part], *done)
    return (grad_query, *done)


def solution(mesh):
    rows = P(("groups", "ctx"), "tp")
    return jax.shard_map(
        per_device,
        mesh=mesh,
        in_specs=(rows, rows, rows, rows, P(("groups", "ctx"), "tp", None, None), P("tp")),
        out_specs=(rows, rows, rows),
        check_vma=False,
    )
```

```python
import functools

import jax
import jax.numpy as jnp
from jax import lax
from jax.experimental import pallas as pl
from jax.experimental.pallas import tpu as pltpu
from jax.sharding import PartitionSpec as P

HEAD = 128
QUAD = 4
SPLIT = (2, 2)
STEPS = (2, 1, 3, 0)
TOKEN = 0
VMEM = pl.BlockSpec(memory_space=pltpu.VMEM)
ANY = pl.BlockSpec(memory_space=pl.ANY)
HBM = pl.BlockSpec(memory_space=pltpu.HBM)
NN = (((1,), (0,)), ((), ()))
NT = (((1,), (1,)), ((), ()))
TN = (((0,), (0,)), ((), ()))


def dot(left, right, dims):
    return lax.dot_general(left, right, dims, preferred_element_type=jnp.float32)


def columns(head, count=1):
    if isinstance(head, int):
        return pl.ds(head * HEAD, count * HEAD)
    return pl.ds(pl.multiple_of(head * HEAD, HEAD), count * HEAD)


def lower(rows):
    row = lax.broadcasted_iota(jnp.int32, (rows, rows), 0)
    return row >= lax.broadcasted_iota(jnp.int32, (rows, rows), 1)


def parts_of(heads):
    each = heads // QUAD
    parts, start = [], 0
    for index, count in enumerate(SPLIT):
        count = each - start if index == len(SPLIT) - 1 else count
        parts.append((start, count))
        start += count
    return each, parts


def forward_kernel(
    q_hbm, k_hbm, v_hbm, s_hbm, y_hbm, gain_hbm,
    out_ref, probs_ref, stat_ref, q_ref, k_ref, v_ref, s_ref, y_ref, gain_ref, sems,
):
    rows, width = q_ref.shape
    pairs = ((q_hbm, q_ref), (k_hbm, k_ref), (v_hbm, v_ref), (s_hbm, s_ref), (gain_hbm, gain_ref))
    pairs += ((y_hbm, y_ref),)
    copies = [
        pltpu.make_async_copy(source, target, sems.at[index])
        for index, (source, target) in enumerate(pairs)
    ]
    for copy in copies:
        copy.start()
    mask = lower(rows)
    heads = [(head, columns(head)) for head in range(width // HEAD)]
    for copy in copies[:2]:
        copy.wait()
    for head, at in heads:
        scores = dot(q_ref[:, at], k_ref[:, at], NT)
        probs_ref[:, at] = jnp.where(mask, scores, 0.0).astype(jnp.bfloat16)
    for copy in copies[2:]:
        copy.wait()
    squares = jnp.zeros((rows, HEAD), jnp.float32)
    crosses = jnp.zeros((rows, HEAD), jnp.float32)
    for head, at in heads:
        out = dot(probs_ref[:, at], v_ref[:, at], NN) + dot(q_ref[:, at], s_ref[head], NN)
        out_ref[:, at] = out
        squares += out * out
        crosses += gain_ref[:, at] * y_ref[:, at].astype(jnp.float32) * out
    lane = lax.broadcasted_iota(jnp.int32, (rows, HEAD), 1)
    square = jnp.sum(squares, axis=1, keepdims=True)
    cross = jnp.sum(crosses, axis=1, keepdims=True)
    stat_ref[...] = jnp.where(lane == 0, square, cross)


def state_kernel(
    features, each, start, count, own_ref, other_ref, out_ref, y_ref, gain_ref, q_ref, *refs
):
    g_ref, *u_refs = refs[-1 - QUAD :]
    stat = own_ref[...] + other_ref[...]
    square, cross = stat[:, 0:1], stat[:, 1:2]
    inverse = lax.rsqrt(square / features + 1e-06)
    back = cross * (inverse * inverse * inverse) / features
    me = lax.rem(lax.axis_index("ctx"), QUAD)
    for index, step in enumerate(STEPS):
        for local in range(count):
            at = columns((me ^ step) * each + start + local)
            weighted = gain_ref[:, at] * y_ref[:, at].astype(jnp.float32)
            grad = (inverse * weighted - out_ref[:, at] * back).astype(jnp.bfloat16)
            g_ref[:, columns(index * count + local)] = grad
            u_refs[index][local] = dot(q_ref[:, at], grad, TN)


def suffix_kernel(*refs):
    block_refs, behind_refs, sum_refs = refs[:QUAD], refs[QUAD:-QUAD], refs[-QUAD:]
    place = lax.axis_index("ctx")
    me = lax.rem(place, QUAD)
    blocks = [ref[...] for ref in block_refs]
    behind = jnp.zeros_like(blocks[0])
    for level, ref in enumerate(behind_refs):
        behind += jnp.where((place & (QUAD << level)) == 0, ref[...], 0.0)
    for target, step in enumerate(STEPS):
        value = behind
        for source, other in enumerate(STEPS):
            if source != target:
                value += jnp.where((me ^ other) > (me ^ step), blocks[source], 0.0)
        sum_refs[target][...] = value


def local_kernel(each, parts, q_ref, k_ref, v_ref, s_ref, probs_ref, *refs):
    g_refs, query_ref = refs[: len(parts)], refs[len(parts)]
    key_refs = refs[len(parts) + 1 : 2 * len(parts) + 1]
    value_refs = refs[2 * len(parts) + 1 :]
    mask = lower(q_ref.shape[0])
    me = lax.rem(lax.axis_index("ctx"), QUAD)
    for part, (start, count) in enumerate(parts):
        for index, step in enumerate(STEPS):
            for local in range(count):
                head = (me ^ step) * each + start + local
                at, slot = columns(head), columns(index * count + local)
                g = g_refs[part][:, slot]
                grads = jnp.where(mask, dot(g, v_ref[:, at], NT), 0.0).astype(jnp.bfloat16)
                query = dot(grads, k_ref[:, at], NN) + dot(g, s_ref[head], NT)
                query_ref[:, at] = query.astype(jnp.bfloat16)
                key_refs[part][:, slot] = dot(grads, q_ref[:, at], TN)
                value_refs[part][:, slot] = dot(probs_ref[:, at], g, TN)


def final_kernel(each, start, count, k_ref, v_ref, key_in, value_in, *refs):
    later_refs = refs[:QUAD]
    key_hbm, value_hbm, key_ref, value_ref, sems = refs[-5:]
    me = lax.rem(lax.axis_index("ctx"), QUAD)
    copies = []
    for index, step in enumerate(STEPS):
        slots = columns(index * count, count)
        for local in range(count):
            at = columns((me ^ step) * each + start + local)
            slot = columns(index * count + local)
            later = later_refs[index][local].astype(jnp.bfloat16)
            key = key_in[:, slot] + dot(v_ref[:, at], later, NT)
            key_ref[:, slot] = key.astype(jnp.bfloat16)
            value = value_in[:, slot] + dot(k_ref[:, at], later, NN)
            value_ref[:, slot] = value.astype(jnp.bfloat16)
        at = columns((me ^ step) * each + start, count)
        for pair, (source, target) in enumerate(((key_ref, key_hbm), (value_ref, value_hbm))):
            copy = pltpu.make_async_copy(source.at[:, slots], target.at[:, at], sems.at[index, pair])
            copy.start()
            copies.append(copy)
    for copy in copies:
        copy.wait()


def params(mib):
    return pltpu.CompilerParams(vmem_limit_bytes=mib << 20)


def partner(value, axis, mask):
    count = lax.axis_size(axis)
    return lax.ppermute(value, axis, [(source, source ^ mask) for source in range(count)])


def quad_swap(pieces):
    return [
        partner(piece, "ctx", step) if step else piece for piece, step in zip(pieces, STEPS)
    ]


def per_device(queries, keys, values, grad_y, state_low, gain):
    rows, width = queries.shape
    heads = width // HEAD
    each, parts = parts_of(heads)
    features = width * lax.axis_size("tp")
    state = state_low[0]
    gain_row = gain.reshape(1, width)

    near = pltpu.VMEM
    half = jax.ShapeDtypeStruct((rows, width), jnp.bfloat16)
    held_half = near((rows, width), jnp.bfloat16)
    operands = (queries, keys, values, state, grad_y, gain_row)
    out, probs, stat, q, k, v, s, y, gain_v = pl.pallas_call(
        forward_kernel,
        out_shape=(
            near((rows, width), jnp.float32),
            held_half,
            near((rows, HEAD), jnp.float32),
            held_half,
            held_half,
            held_half,
            near(state.shape, state.dtype),
            held_half,
            near(gain_row.shape, gain_row.dtype),
        ),
        in_specs=[HBM] * 6,
        out_specs=(VMEM,) * 9,
        scratch_shapes=[pltpu.SemaphoreType.DMA((6,))],
        compiler_params=params(8),
    )(*(pltpu.with_memory_space_constraint(value, pltpu.HBM) for value in operands))
    other = partner(stat, "tp", 1)

    grads, held = [], []
    for start, count in parts:
        tokens = [held[-1][TOKEN]] if held else []
        piece = near((count, HEAD, HEAD), jnp.float32)
        grad, *own = pl.pallas_call(
            functools.partial(state_kernel, features, each, start, count),
            out_shape=(near((rows, QUAD * count * HEAD), jnp.bfloat16),) + (piece,) * QUAD,
            in_specs=[VMEM] * 6 + [ANY] * len(tokens),
            out_specs=(VMEM,) * (1 + QUAD),
            compiler_params=params(8),
        )(stat, other, out, y, gain_v, q, *tokens)
        grads.append(grad)
        held.append(quad_swap(own))
    later = []
    for blocks in held:
        total = blocks[0] + blocks[1] + blocks[2] + blocks[3]
        behind = []
        span = QUAD
        while span < lax.axis_size("ctx"):
            behind.append(partner(total, "ctx", span))
            span *= 2
            if span < lax.axis_size("ctx"):
                total = total + behind[-1]
        piece = near(total.shape, jnp.float32)
        sums = pl.pallas_call(
            suffix_kernel,
            out_shape=(piece,) * QUAD,
            in_specs=[VMEM] * (QUAD + len(behind)),
            out_specs=(VMEM,) * QUAD,
            compiler_params=params(8),
        )(*blocks, *behind)
        later.append(quad_swap(sums))

    slots = [near((rows, QUAD * count * HEAD), jnp.float32) for _, count in parts]
    grad_query, *local = pl.pallas_call(
        functools.partial(local_kernel, each, parts),
        out_shape=(half, *slots, *slots),
        in_specs=[VMEM] * (5 + len(parts)),
        out_specs=(VMEM,) * (1 + 2 * len(parts)),
        compiler_params=params(8),
    )(q, k, v, s, probs, *grads)
    done = ()
    for part, (start, count) in enumerate(parts):
        stage = pltpu.VMEM((rows, QUAD * count * HEAD), jnp.bfloat16)
        done = pl.pallas_call(
            functools.partial(final_kernel, each, start, count),
            out_shape=(half, half),
            in_specs=[VMEM] * (4 + QUAD) + [HBM] * len(done),
            out_specs=(HBM,) * 2,
            scratch_shapes=[stage, stage, pltpu.SemaphoreType.DMA((QUAD, 2))],
            input_output_aliases={4 + QUAD + index: index for index in range(len(done))},
            compiler_params=params(8),
        )(k, v, local[part], local[len(parts) + part], *later[part], *done)
    return (grad_query, *done)


def solution(mesh):
    rows = P(("groups", "ctx"), "tp")
    return jax.shard_map(
        per_device,
        mesh=mesh,
        in_specs=(rows, rows, rows, rows, P(("groups", "ctx"), "tp", None, None), P("tp")),
        out_specs=(rows, rows, rows),
        check_vma=False,
    )
```

```python
import functools

import jax
import jax.numpy as jnp
from jax import lax
from jax.experimental import pallas as pl
from jax.experimental.pallas import tpu as pltpu
from jax.sharding import PartitionSpec as P

HEAD = 128
QUAD = 4
SPLIT = (2, 2)
STEPS = (2, 1, 3, 0)
FINALS = ((0, (2, 1, 3, 0)), (1, (0, 2, 1)), (1, (3,)))
CALLS = (
    (((0, 1), (0, 2), (0, 3), (0, 0)), None),
    (((1, 3), (1, 2), (1, 1), (1, 0)), (0, 2)),
)
VMEM = pl.BlockSpec(memory_space=pltpu.VMEM)
ANY = pl.BlockSpec(memory_space=pl.ANY)
HBM = pl.BlockSpec(memory_space=pltpu.HBM)
NN = (((1,), (0,)), ((), ()))
NT = (((1,), (1,)), ((), ()))
TN = (((0,), (0,)), ((), ()))


def dot(left, right, dims):
    return lax.dot_general(left, right, dims, preferred_element_type=jnp.float32)


def columns(head, count=1):
    if isinstance(head, int):
        return pl.ds(head * HEAD, count * HEAD)
    return pl.ds(pl.multiple_of(head * HEAD, HEAD), count * HEAD)


def lower(rows):
    row = lax.broadcasted_iota(jnp.int32, (rows, rows), 0)
    return row >= lax.broadcasted_iota(jnp.int32, (rows, rows), 1)


def parts_of(heads):
    each = heads // QUAD
    parts, start = [], 0
    for index, count in enumerate(SPLIT):
        count = each - start if index == len(SPLIT) - 1 else count
        parts.append((start, count))
        start += count
    return each, parts


def forward_kernel(
    q_hbm, k_hbm, v_hbm, s_hbm, y_hbm, gain_hbm,
    out_ref, probs_ref, stat_ref, q_ref, k_ref, v_ref, s_ref, y_ref, gain_ref, sems,
):
    rows, width = q_ref.shape
    pairs = ((q_hbm, q_ref), (k_hbm, k_ref), (v_hbm, v_ref), (s_hbm, s_ref), (gain_hbm, gain_ref))
    pairs += ((y_hbm, y_ref),)
    copies = [
        pltpu.make_async_copy(source, target, sems.at[index])
        for index, (source, target) in enumerate(pairs)
    ]
    for copy in copies:
        copy.start()
    mask = lower(rows)
    heads = [(head, columns(head)) for head in range(width // HEAD)]
    for copy in copies[:2]:
        copy.wait()
    for head, at in heads:
        scores = dot(q_ref[:, at], k_ref[:, at], NT)
        probs_ref[:, at] = jnp.where(mask, scores, 0.0).astype(jnp.bfloat16)
    for copy in copies[2:]:
        copy.wait()
    squares = jnp.zeros((rows, HEAD), jnp.float32)
    crosses = jnp.zeros((rows, HEAD), jnp.float32)
    for head, at in heads:
        out = dot(probs_ref[:, at], v_ref[:, at], NN) + dot(q_ref[:, at], s_ref[head], NN)
        out_ref[:, at] = out
        squares += out * out
        crosses += gain_ref[:, at] * y_ref[:, at].astype(jnp.float32) * out
    lane = lax.broadcasted_iota(jnp.int32, (rows, HEAD), 1)
    square = jnp.sum(squares, axis=1, keepdims=True)
    cross = jnp.sum(crosses, axis=1, keepdims=True)
    stat_ref[...] = jnp.where(lane == 0, square, cross)


def state_kernel(features, each, parts, pieces, own_ref, other_ref, out_ref, y_ref, gain_ref, q_ref, *refs):
    g_ref, *u_refs = refs[-1 - len(pieces) :]
    stat = own_ref[...] + other_ref[...]
    square, cross = stat[:, 0:1], stat[:, 1:2]
    inverse = lax.rsqrt(square / features + 1e-06)
    back = cross * (inverse * inverse * inverse) / features
    me = lax.rem(lax.axis_index("ctx"), QUAD)
    slot = 0
    for (part, step), u_ref in zip(pieces, u_refs):
        start, count = parts[part]
        for local in range(count):
            at = columns((me ^ step) * each + start + local)
            weighted = gain_ref[:, at] * y_ref[:, at].astype(jnp.float32)
            grad = (inverse * weighted - out_ref[:, at] * back).astype(jnp.bfloat16)
            g_ref[:, columns(slot)] = grad
            slot += 1
            u_ref[local] = dot(q_ref[:, at], grad, TN)


def suffix_kernel(*refs):
    block_refs, behind_refs, sum_refs = refs[:QUAD], refs[QUAD:-QUAD], refs[-QUAD:]
    place = lax.axis_index("ctx")
    me = lax.rem(place, QUAD)
    blocks = [ref[...] for ref in block_refs]
    behind = jnp.zeros_like(blocks[0])
    for level, ref in enumerate(behind_refs):
        behind += jnp.where((place & (QUAD << level)) == 0, ref[...], 0.0)
    for target, step in enumerate(STEPS):
        value = behind
        for source, other in enumerate(STEPS):
            if source != target:
                value += jnp.where((me ^ other) > (me ^ step), blocks[source], 0.0)
        sum_refs[target][...] = value


def local_kernel(each, parts, q_ref, k_ref, v_ref, s_ref, probs_ref, *refs):
    g_refs, query_ref = refs[: len(CALLS)], refs[len(CALLS)]
    key_refs = refs[len(CALLS) + 1 : len(CALLS) + 1 + len(parts)]
    value_refs = refs[len(CALLS) + 1 + len(parts) :]
    mask = lower(q_ref.shape[0])
    me = lax.rem(lax.axis_index("ctx"), QUAD)
    for (pieces, _), g_ref in zip(CALLS, g_refs):
        place = 0
        for part, step in pieces:
            start, count = parts[part]
            for local in range(count):
                head = (me ^ step) * each + start + local
                at, slot = columns(head), columns(STEPS.index(step) * count + local)
                g = g_ref[:, columns(place)]
                place += 1
                grads = jnp.where(mask, dot(g, v_ref[:, at], NT), 0.0).astype(jnp.bfloat16)
                query = dot(grads, k_ref[:, at], NN) + dot(g, s_ref[head], NT)
                query_ref[:, at] = query.astype(jnp.bfloat16)
                key_refs[part][:, slot] = dot(grads, q_ref[:, at], TN)
                value_refs[part][:, slot] = dot(probs_ref[:, at], g, TN)


def final_kernel(each, start, count, steps, k_ref, v_ref, key_in, value_in, *refs):
    later_refs = refs[: len(steps)]
    key_hbm, value_hbm, key_ref, value_ref, sems = refs[-5:]
    me = lax.rem(lax.axis_index("ctx"), QUAD)
    copies = []
    for index, step in enumerate(steps):
        for local in range(count):
            at = columns((me ^ step) * each + start + local)
            source = columns(STEPS.index(step) * count + local)
            slot = columns(index * count + local)
            later = later_refs[index][local].astype(jnp.bfloat16)
            key = key_in[:, source] + dot(v_ref[:, at], later, NT)
            key_ref[:, slot] = key.astype(jnp.bfloat16)
            value = value_in[:, source] + dot(k_ref[:, at], later, NN)
            value_ref[:, slot] = value.astype(jnp.bfloat16)
        slots = columns(index * count, count)
        at = columns((me ^ step) * each + start, count)
        for pair, (source, target) in enumerate(((key_ref, key_hbm), (value_ref, value_hbm))):
            copy = pltpu.make_async_copy(source.at[:, slots], target.at[:, at], sems.at[index, pair])
            copy.start()
            copies.append(copy)
    for copy in copies:
        copy.wait()


def params(mib):
    return pltpu.CompilerParams(vmem_limit_bytes=mib << 20)


def partner(value, axis, mask):
    count = lax.axis_size(axis)
    return lax.ppermute(value, axis, [(source, source ^ mask) for source in range(count)])


def quad_swap(pieces):
    return [
        partner(piece, "ctx", step) if step else piece for piece, step in zip(pieces, STEPS)
    ]


def per_device(queries, keys, values, grad_y, state_low, gain):
    rows, width = queries.shape
    heads = width // HEAD
    each, parts = parts_of(heads)
    features = width * lax.axis_size("tp")
    state = state_low[0]
    gain_row = gain.reshape(1, width)

    near = pltpu.VMEM
    half = jax.ShapeDtypeStruct((rows, width), jnp.bfloat16)
    held_half = near((rows, width), jnp.bfloat16)
    operands = (queries, keys, values, state, grad_y, gain_row)
    out, probs, stat, q, k, v, s, y, gain_v = pl.pallas_call(
        forward_kernel,
        out_shape=(
            near((rows, width), jnp.float32),
            held_half,
            near((rows, HEAD), jnp.float32),
            held_half,
            held_half,
            held_half,
            near(state.shape, state.dtype),
            held_half,
            near(gain_row.shape, gain_row.dtype),
        ),
        in_specs=[HBM] * 6,
        out_specs=(VMEM,) * 9,
        scratch_shapes=[pltpu.SemaphoreType.DMA((6,))],
        compiler_params=params(8),
    )(*(pltpu.with_memory_space_constraint(value, pltpu.HBM) for value in operands))
    other = partner(stat, "tp", 1)

    grads, found = [], {}
    for pieces, token in CALLS:
        tokens = [found[token]] if token else []
        shapes = [near((parts[part][1], HEAD, HEAD), jnp.float32) for part, _ in pieces]
        wide = sum(shape.shape[0] for shape in shapes) * HEAD
        grad, *own = pl.pallas_call(
            functools.partial(state_kernel, features, each, parts, pieces),
            out_shape=(near((rows, wide), jnp.bfloat16), *shapes),
            in_specs=[VMEM] * 6 + [ANY] * len(tokens),
            out_specs=(VMEM,) * (1 + len(pieces)),
            compiler_params=params(8),
        )(stat, other, out, y, gain_v, q, *tokens)
        grads.append(grad)
        for (part, step), piece in zip(pieces, own):
            found[part, step] = partner(piece, "ctx", step) if step else piece
    held = [[found[part, step] for step in STEPS] for part in range(len(parts))]
    later = []
    for blocks in held:
        total = blocks[0] + blocks[1] + blocks[2] + blocks[3]
        behind = []
        span = QUAD
        while span < lax.axis_size("ctx"):
            behind.append(partner(total, "ctx", span))
            span *= 2
            if span < lax.axis_size("ctx"):
                total = total + behind[-1]
        piece = near(total.shape, jnp.float32)
        sums = pl.pallas_call(
            suffix_kernel,
            out_shape=(piece,) * QUAD,
            in_specs=[VMEM] * (QUAD + len(behind)),
            out_specs=(VMEM,) * QUAD,
            compiler_params=params(8),
        )(*blocks, *behind)
        later.append(quad_swap(sums))

    slots = [near((rows, QUAD * count * HEAD), jnp.float32) for _, count in parts]
    grad_query, *local = pl.pallas_call(
        functools.partial(local_kernel, each, parts),
        out_shape=(half, *slots, *slots),
        in_specs=[VMEM] * (5 + len(grads)),
        out_specs=(VMEM,) * (1 + 2 * len(parts)),
        compiler_params=params(8),
    )(q, k, v, s, probs, *grads)
    done = ()
    for part, steps in FINALS:
        start, count = parts[part]
        stage = pltpu.VMEM((rows, len(steps) * count * HEAD), jnp.bfloat16)
        pieces = [later[part][STEPS.index(step)] for step in steps]
        done = pl.pallas_call(
            functools.partial(final_kernel, each, start, count, steps),
            out_shape=(half, half),
            in_specs=[VMEM] * (4 + len(steps)) + [HBM] * len(done),
            out_specs=(HBM,) * 2,
            scratch_shapes=[stage, stage, pltpu.SemaphoreType.DMA((QUAD, 2))],
            input_output_aliases={4 + len(steps) + index: index for index in range(len(done))},
            compiler_params=params(8),
        )(k, v, local[part], local[len(parts) + part], *pieces, *done)
    return (grad_query, *done)


def solution(mesh):
    rows = P(("groups", "ctx"), "tp")
    return jax.shard_map(
        per_device,
        mesh=mesh,
        in_specs=(rows, rows, rows, rows, P(("groups", "ctx"), "tp", None, None), P("tp")),
        out_specs=(rows, rows, rows),
        check_vma=False,
    )
```

```python
import functools

import jax
import jax.numpy as jnp
from jax import lax
from jax.experimental import pallas as pl
from jax.experimental.pallas import tpu as pltpu
from jax.sharding import PartitionSpec as P

HEAD = 128
QUAD = 4
SPLIT = (2, 2)
STEPS = (2, 1, 3, 0)
TOKEN = 0
VMEM = pl.BlockSpec(memory_space=pltpu.VMEM)
ANY = pl.BlockSpec(memory_space=pl.ANY)
HBM = pl.BlockSpec(memory_space=pltpu.HBM)
NN = (((1,), (0,)), ((), ()))
NT = (((1,), (1,)), ((), ()))
TN = (((0,), (0,)), ((), ()))


def dot(left, right, dims):
    return lax.dot_general(left, right, dims, preferred_element_type=jnp.float32)


def columns(head, count=1):
    if isinstance(head, int):
        return pl.ds(head * HEAD, count * HEAD)
    return pl.ds(pl.multiple_of(head * HEAD, HEAD), count * HEAD)


def turn(step):
    core = lax.rem(lax.axis_index("tp"), 2)
    return {0: 0, 1: 1 + core, 2: 2 - core, 3: 3}[step]


def lower(rows):
    row = lax.broadcasted_iota(jnp.int32, (rows, rows), 0)
    return row >= lax.broadcasted_iota(jnp.int32, (rows, rows), 1)


def parts_of(heads):
    each = heads // QUAD
    parts, start = [], 0
    for index, count in enumerate(SPLIT):
        count = each - start if index == len(SPLIT) - 1 else count
        parts.append((start, count))
        start += count
    return each, parts


def forward_kernel(
    q_hbm, k_hbm, v_hbm, s_hbm, y_hbm, gain_hbm,
    out_ref, probs_ref, stat_ref, q_ref, k_ref, v_ref, s_ref, y_ref, gain_ref, sems,
):
    rows, width = q_ref.shape
    pairs = ((q_hbm, q_ref), (k_hbm, k_ref), (v_hbm, v_ref), (s_hbm, s_ref), (gain_hbm, gain_ref))
    pairs += ((y_hbm, y_ref),)
    copies = [
        pltpu.make_async_copy(source, target, sems.at[index])
        for index, (source, target) in enumerate(pairs)
    ]
    for copy in copies:
        copy.start()
    mask = lower(rows)
    heads = [(head, columns(head)) for head in range(width // HEAD)]
    for copy in copies[:2]:
        copy.wait()
    for head, at in heads:
        scores = dot(q_ref[:, at], k_ref[:, at], NT)
        probs_ref[:, at] = jnp.where(mask, scores, 0.0).astype(jnp.bfloat16)
    for copy in copies[2:]:
        copy.wait()
    squares = jnp.zeros((rows, HEAD), jnp.float32)
    crosses = jnp.zeros((rows, HEAD), jnp.float32)
    for head, at in heads:
        out = dot(probs_ref[:, at], v_ref[:, at], NN) + dot(q_ref[:, at], s_ref[head], NN)
        out_ref[:, at] = out
        squares += out * out
        crosses += gain_ref[:, at] * y_ref[:, at].astype(jnp.float32) * out
    lane = lax.broadcasted_iota(jnp.int32, (rows, HEAD), 1)
    square = jnp.sum(squares, axis=1, keepdims=True)
    cross = jnp.sum(crosses, axis=1, keepdims=True)
    stat_ref[...] = jnp.where(lane == 0, square, cross)


def state_kernel(
    features, each, start, count, own_ref, other_ref, out_ref, y_ref, gain_ref, q_ref, *refs
):
    g_ref, *u_refs = refs[-1 - QUAD :]
    stat = own_ref[...] + other_ref[...]
    square, cross = stat[:, 0:1], stat[:, 1:2]
    inverse = lax.rsqrt(square / features + 1e-06)
    back = cross * (inverse * inverse * inverse) / features
    me = lax.rem(lax.axis_index("ctx"), QUAD)
    for index, step in enumerate(STEPS):
        for local in range(count):
            at = columns((me ^ step) * each + start + local)
            weighted = gain_ref[:, at] * y_ref[:, at].astype(jnp.float32)
            grad = (inverse * weighted - out_ref[:, at] * back).astype(jnp.bfloat16)
            g_ref[:, columns(index * count + local)] = grad
            u_refs[index][local] = dot(q_ref[:, at], grad, TN)


def suffix_kernel(*refs):
    block_refs, behind_refs, sum_refs = refs[:QUAD], refs[QUAD:-QUAD], refs[-QUAD:]
    place = lax.axis_index("ctx")
    me = lax.rem(place, QUAD)
    blocks = [ref[...] for ref in block_refs]
    behind = jnp.zeros_like(blocks[0])
    for level, ref in enumerate(behind_refs):
        behind += jnp.where((place & (QUAD << level)) == 0, ref[...], 0.0)
    for target, step in enumerate(STEPS):
        value = behind
        for source, other in enumerate(STEPS):
            value += jnp.where((me ^ other) > (me ^ turn(step)), blocks[source], 0.0)
        sum_refs[target][...] = value


def local_kernel(each, parts, q_ref, k_ref, v_ref, s_ref, probs_ref, *refs):
    g_refs, query_ref = refs[: len(parts)], refs[len(parts)]
    key_refs = refs[len(parts) + 1 : 2 * len(parts) + 1]
    value_refs = refs[2 * len(parts) + 1 :]
    mask = lower(q_ref.shape[0])
    me = lax.rem(lax.axis_index("ctx"), QUAD)
    for part, (start, count) in enumerate(parts):
        for index, step in enumerate(STEPS):
            for local in range(count):
                head = (me ^ turn(step)) * each + start + local
                at, slot = columns(head), columns(index * count + local)
                held = index if index > 1 else lax.rem(lax.axis_index("tp") + index, 2)
                g = g_refs[part][:, columns(held * count + local)]
                grads = jnp.where(mask, dot(g, v_ref[:, at], NT), 0.0).astype(jnp.bfloat16)
                query = dot(grads, k_ref[:, at], NN) + dot(g, s_ref[head], NT)
                query_ref[:, at] = query.astype(jnp.bfloat16)
                key_refs[part][:, slot] = dot(grads, q_ref[:, at], TN)
                value_refs[part][:, slot] = dot(probs_ref[:, at], g, TN)


def final_kernel(each, start, count, k_ref, v_ref, key_in, value_in, *refs):
    later_refs = refs[:QUAD]
    key_hbm, value_hbm, key_ref, value_ref, sems = refs[-5:]
    me = lax.rem(lax.axis_index("ctx"), QUAD)
    copies = []
    for index, step in enumerate(STEPS):
        slots = columns(index * count, count)
        for local in range(count):
            at = columns((me ^ turn(step)) * each + start + local)
            slot = columns(index * count + local)
            later = later_refs[index][local].astype(jnp.bfloat16)
            key = key_in[:, slot] + dot(v_ref[:, at], later, NT)
            key_ref[:, slot] = key.astype(jnp.bfloat16)
            value = value_in[:, slot] + dot(k_ref[:, at], later, NN)
            value_ref[:, slot] = value.astype(jnp.bfloat16)
        at = columns((me ^ turn(step)) * each + start, count)
        for pair, (source, target) in enumerate(((key_ref, key_hbm), (value_ref, value_hbm))):
            copy = pltpu.make_async_copy(source.at[:, slots], target.at[:, at], sems.at[index, pair])
            copy.start()
            copies.append(copy)
    for copy in copies:
        copy.wait()


def params(mib):
    return pltpu.CompilerParams(vmem_limit_bytes=mib << 20)


def partner(value, axis, mask):
    count = lax.axis_size(axis)
    return lax.ppermute(value, axis, [(source, source ^ mask) for source in range(count)])


def quad_swap(pieces):
    return [
        partner(piece, "ctx", step) if step else piece for piece, step in zip(pieces, STEPS)
    ]


def return_swap(pieces):
    cores = lax.axis_size("tp")
    places = range(lax.axis_size("ctx"))
    came = []
    for piece, step in zip(pieces, STEPS):
        pairs = []
        for place in places:
            for core in range(cores):
                other = {0: 0, 1: 1 + core % 2, 2: 2 - core % 2, 3: 3}[step]
                pairs.append((place * cores + core, (place ^ other) * cores + core))
        came.append(lax.ppermute(piece, ("ctx", "tp"), pairs) if step else piece)
    return came


def per_device(queries, keys, values, grad_y, state_low, gain):
    rows, width = queries.shape
    heads = width // HEAD
    each, parts = parts_of(heads)
    features = width * lax.axis_size("tp")
    state = state_low[0]
    gain_row = gain.reshape(1, width)

    near = pltpu.VMEM
    half = jax.ShapeDtypeStruct((rows, width), jnp.bfloat16)
    held_half = near((rows, width), jnp.bfloat16)
    operands = (queries, keys, values, state, grad_y, gain_row)
    out, probs, stat, q, k, v, s, y, gain_v = pl.pallas_call(
        forward_kernel,
        out_shape=(
            near((rows, width), jnp.float32),
            held_half,
            near((rows, HEAD), jnp.float32),
            held_half,
            held_half,
            held_half,
            near(state.shape, state.dtype),
            held_half,
            near(gain_row.shape, gain_row.dtype),
        ),
        in_specs=[HBM] * 6,
        out_specs=(VMEM,) * 9,
        scratch_shapes=[pltpu.SemaphoreType.DMA((6,))],
        compiler_params=params(8),
    )(*(pltpu.with_memory_space_constraint(value, pltpu.HBM) for value in operands))
    other = partner(stat, "tp", 1)

    grads, held = [], []
    for start, count in parts:
        tokens = [held[-1][TOKEN]] if held else []
        piece = near((count, HEAD, HEAD), jnp.float32)
        grad, *own = pl.pallas_call(
            functools.partial(state_kernel, features, each, start, count),
            out_shape=(near((rows, QUAD * count * HEAD), jnp.bfloat16),) + (piece,) * QUAD,
            in_specs=[VMEM] * 6 + [ANY] * len(tokens),
            out_specs=(VMEM,) * (1 + QUAD),
            compiler_params=params(8),
        )(stat, other, out, y, gain_v, q, *tokens)
        grads.append(grad)
        held.append(quad_swap(own))
    later = []
    for blocks in held:
        total = blocks[0] + blocks[1] + blocks[2] + blocks[3]
        behind = []
        span = QUAD
        while span < lax.axis_size("ctx"):
            behind.append(partner(total, "ctx", span))
            span *= 2
            if span < lax.axis_size("ctx"):
                total = total + behind[-1]
        piece = near(total.shape, jnp.float32)
        sums = pl.pallas_call(
            suffix_kernel,
            out_shape=(piece,) * QUAD,
            in_specs=[VMEM] * (QUAD + len(behind)),
            out_specs=(VMEM,) * QUAD,
            compiler_params=params(8),
        )(*blocks, *behind)
        later.append(return_swap(sums))

    slots = [near((rows, QUAD * count * HEAD), jnp.float32) for _, count in parts]
    grad_query, *local = pl.pallas_call(
        functools.partial(local_kernel, each, parts),
        out_shape=(half, *slots, *slots),
        in_specs=[VMEM] * (5 + len(parts)),
        out_specs=(VMEM,) * (1 + 2 * len(parts)),
        compiler_params=params(8),
    )(q, k, v, s, probs, *grads)
    done = ()
    for part, (start, count) in enumerate(parts):
        stage = pltpu.VMEM((rows, QUAD * count * HEAD), jnp.bfloat16)
        done = pl.pallas_call(
            functools.partial(final_kernel, each, start, count),
            out_shape=(half, half),
            in_specs=[VMEM] * (4 + QUAD) + [HBM] * len(done),
            out_specs=(HBM,) * 2,
            scratch_shapes=[stage, stage, pltpu.SemaphoreType.DMA((QUAD, 2))],
            input_output_aliases={4 + QUAD + index: index for index in range(len(done))},
            compiler_params=params(8),
        )(k, v, local[part], local[len(parts) + part], *later[part], *done)
    return (grad_query, *done)


def solution(mesh):
    rows = P(("groups", "ctx"), "tp")
    return jax.shard_map(
        per_device,
        mesh=mesh,
        in_specs=(rows, rows, rows, rows, P(("groups", "ctx"), "tp", None, None), P("tp")),
        out_specs=(rows, rows, rows),
        check_vma=False,
    )
```

```python
import functools

import jax
import jax.numpy as jnp
from jax import lax
from jax.experimental import pallas as pl
from jax.experimental.pallas import tpu as pltpu
from jax.sharding import PartitionSpec as P

HEAD = 128
QUAD = 4
SPLIT = (2, 2)
STEPS = (2, 1, 3, 0)
CALLS = (
    (((0, 2),), None),
    (((0, 1), (0, 3), (0, 0)), None),
    (((1, 2), (1, 1), (1, 3), (1, 0)), (0, 2)),
)
VMEM = pl.BlockSpec(memory_space=pltpu.VMEM)
ANY = pl.BlockSpec(memory_space=pl.ANY)
HBM = pl.BlockSpec(memory_space=pltpu.HBM)
NN = (((1,), (0,)), ((), ()))
NT = (((1,), (1,)), ((), ()))
TN = (((0,), (0,)), ((), ()))


def dot(left, right, dims):
    return lax.dot_general(left, right, dims, preferred_element_type=jnp.float32)


def columns(head, count=1):
    if isinstance(head, int):
        return pl.ds(head * HEAD, count * HEAD)
    return pl.ds(pl.multiple_of(head * HEAD, HEAD), count * HEAD)


def lower(rows):
    row = lax.broadcasted_iota(jnp.int32, (rows, rows), 0)
    return row >= lax.broadcasted_iota(jnp.int32, (rows, rows), 1)


def parts_of(heads):
    each = heads // QUAD
    parts, start = [], 0
    for index, count in enumerate(SPLIT):
        count = each - start if index == len(SPLIT) - 1 else count
        parts.append((start, count))
        start += count
    return each, parts


def forward_kernel(
    q_hbm, k_hbm, v_hbm, s_hbm, y_hbm, gain_hbm,
    out_ref, probs_ref, stat_ref, q_ref, k_ref, v_ref, s_ref, y_ref, gain_ref, sems,
):
    rows, width = q_ref.shape
    pairs = ((q_hbm, q_ref), (k_hbm, k_ref), (v_hbm, v_ref), (s_hbm, s_ref), (gain_hbm, gain_ref))
    pairs += ((y_hbm, y_ref),)
    copies = [
        pltpu.make_async_copy(source, target, sems.at[index])
        for index, (source, target) in enumerate(pairs)
    ]
    for copy in copies:
        copy.start()
    mask = lower(rows)
    heads = [(head, columns(head)) for head in range(width // HEAD)]
    for copy in copies[:2]:
        copy.wait()
    for head, at in heads:
        scores = dot(q_ref[:, at], k_ref[:, at], NT)
        probs_ref[:, at] = jnp.where(mask, scores, 0.0).astype(jnp.bfloat16)
    for copy in copies[2:]:
        copy.wait()
    squares = jnp.zeros((rows, HEAD), jnp.float32)
    crosses = jnp.zeros((rows, HEAD), jnp.float32)
    for head, at in heads:
        out = dot(probs_ref[:, at], v_ref[:, at], NN) + dot(q_ref[:, at], s_ref[head], NN)
        out_ref[:, at] = out
        squares += out * out
        crosses += gain_ref[:, at] * y_ref[:, at].astype(jnp.float32) * out
    lane = lax.broadcasted_iota(jnp.int32, (rows, HEAD), 1)
    square = jnp.sum(squares, axis=1, keepdims=True)
    cross = jnp.sum(crosses, axis=1, keepdims=True)
    stat_ref[...] = jnp.where(lane == 0, square, cross)


def state_kernel(features, each, parts, pieces, own_ref, other_ref, out_ref, y_ref, gain_ref, q_ref, *refs):
    g_ref, *u_refs = refs[-1 - len(pieces) :]
    stat = own_ref[...] + other_ref[...]
    square, cross = stat[:, 0:1], stat[:, 1:2]
    inverse = lax.rsqrt(square / features + 1e-06)
    back = cross * (inverse * inverse * inverse) / features
    me = lax.rem(lax.axis_index("ctx"), QUAD)
    slot = 0
    for (part, step), u_ref in zip(pieces, u_refs):
        start, count = parts[part]
        for local in range(count):
            at = columns((me ^ step) * each + start + local)
            weighted = gain_ref[:, at] * y_ref[:, at].astype(jnp.float32)
            grad = (inverse * weighted - out_ref[:, at] * back).astype(jnp.bfloat16)
            g_ref[:, columns(slot)] = grad
            slot += 1
            u_ref[local] = dot(q_ref[:, at], grad, TN)


def suffix_kernel(*refs):
    block_refs, behind_refs, sum_refs = refs[:QUAD], refs[QUAD:-QUAD], refs[-QUAD:]
    place = lax.axis_index("ctx")
    me = lax.rem(place, QUAD)
    blocks = [ref[...] for ref in block_refs]
    behind = jnp.zeros_like(blocks[0])
    for level, ref in enumerate(behind_refs):
        behind += jnp.where((place & (QUAD << level)) == 0, ref[...], 0.0)
    for target, step in enumerate(STEPS):
        value = behind
        for source, other in enumerate(STEPS):
            if source != target:
                value += jnp.where((me ^ other) > (me ^ step), blocks[source], 0.0)
        sum_refs[target][...] = value


def local_kernel(each, parts, q_ref, k_ref, v_ref, s_ref, probs_ref, *refs):
    g_refs, query_ref = refs[: len(CALLS)], refs[len(CALLS)]
    key_refs = refs[len(CALLS) + 1 : len(CALLS) + 1 + len(parts)]
    value_refs = refs[len(CALLS) + 1 + len(parts) :]
    mask = lower(q_ref.shape[0])
    me = lax.rem(lax.axis_index("ctx"), QUAD)
    for (pieces, _), g_ref in zip(CALLS, g_refs):
        place = 0
        for part, step in pieces:
            start, count = parts[part]
            for local in range(count):
                head = (me ^ step) * each + start + local
                at, slot = columns(head), columns(STEPS.index(step) * count + local)
                g = g_ref[:, columns(place)]
                place += 1
                grads = jnp.where(mask, dot(g, v_ref[:, at], NT), 0.0).astype(jnp.bfloat16)
                query = dot(grads, k_ref[:, at], NN) + dot(g, s_ref[head], NT)
                query_ref[:, at] = query.astype(jnp.bfloat16)
                key_refs[part][:, slot] = dot(grads, q_ref[:, at], TN)
                value_refs[part][:, slot] = dot(probs_ref[:, at], g, TN)


def final_kernel(each, start, count, k_ref, v_ref, key_in, value_in, *refs):
    later_refs = refs[:QUAD]
    key_hbm, value_hbm, key_ref, value_ref, sems = refs[-5:]
    me = lax.rem(lax.axis_index("ctx"), QUAD)
    copies = []
    for index, step in enumerate(STEPS):
        slots = columns(index * count, count)
        for local in range(count):
            at = columns((me ^ step) * each + start + local)
            slot = columns(index * count + local)
            later = later_refs[index][local].astype(jnp.bfloat16)
            key = key_in[:, slot] + dot(v_ref[:, at], later, NT)
            key_ref[:, slot] = key.astype(jnp.bfloat16)
            value = value_in[:, slot] + dot(k_ref[:, at], later, NN)
            value_ref[:, slot] = value.astype(jnp.bfloat16)
        at = columns((me ^ step) * each + start, count)
        for pair, (source, target) in enumerate(((key_ref, key_hbm), (value_ref, value_hbm))):
            copy = pltpu.make_async_copy(source.at[:, slots], target.at[:, at], sems.at[index, pair])
            copy.start()
            copies.append(copy)
    for copy in copies:
        copy.wait()


def params(mib):
    return pltpu.CompilerParams(vmem_limit_bytes=mib << 20)


def partner(value, axis, mask):
    count = lax.axis_size(axis)
    return lax.ppermute(value, axis, [(source, source ^ mask) for source in range(count)])


def quad_swap(pieces):
    return [
        partner(piece, "ctx", step) if step else piece for piece, step in zip(pieces, STEPS)
    ]


def per_device(queries, keys, values, grad_y, state_low, gain):
    rows, width = queries.shape
    heads = width // HEAD
    each, parts = parts_of(heads)
    features = width * lax.axis_size("tp")
    state = state_low[0]
    gain_row = gain.reshape(1, width)

    near = pltpu.VMEM
    half = jax.ShapeDtypeStruct((rows, width), jnp.bfloat16)
    held_half = near((rows, width), jnp.bfloat16)
    operands = (queries, keys, values, state, grad_y, gain_row)
    out, probs, stat, q, k, v, s, y, gain_v = pl.pallas_call(
        forward_kernel,
        out_shape=(
            near((rows, width), jnp.float32),
            held_half,
            near((rows, HEAD), jnp.float32),
            held_half,
            held_half,
            held_half,
            near(state.shape, state.dtype),
            held_half,
            near(gain_row.shape, gain_row.dtype),
        ),
        in_specs=[HBM] * 6,
        out_specs=(VMEM,) * 9,
        scratch_shapes=[pltpu.SemaphoreType.DMA((6,))],
        compiler_params=params(8),
    )(*(pltpu.with_memory_space_constraint(value, pltpu.HBM) for value in operands))
    other = partner(stat, "tp", 1)

    grads, found = [], {}
    for pieces, token in CALLS:
        tokens = [found[token]] if token else []
        shapes = [near((parts[part][1], HEAD, HEAD), jnp.float32) for part, _ in pieces]
        wide = sum(shape.shape[0] for shape in shapes) * HEAD
        grad, *own = pl.pallas_call(
            functools.partial(state_kernel, features, each, parts, pieces),
            out_shape=(near((rows, wide), jnp.bfloat16), *shapes),
            in_specs=[VMEM] * 6 + [ANY] * len(tokens),
            out_specs=(VMEM,) * (1 + len(pieces)),
            compiler_params=params(8),
        )(stat, other, out, y, gain_v, q, *tokens)
        grads.append(grad)
        for (part, step), piece in zip(pieces, own):
            found[part, step] = partner(piece, "ctx", step) if step else piece
    held = [[found[part, step] for step in STEPS] for part in range(len(parts))]
    later = []
    for blocks in held:
        total = blocks[0] + blocks[1] + blocks[2] + blocks[3]
        behind = []
        span = QUAD
        while span < lax.axis_size("ctx"):
            behind.append(partner(total, "ctx", span))
            span *= 2
            if span < lax.axis_size("ctx"):
                total = total + behind[-1]
        piece = near(total.shape, jnp.float32)
        sums = pl.pallas_call(
            suffix_kernel,
            out_shape=(piece,) * QUAD,
            in_specs=[VMEM] * (QUAD + len(behind)),
            out_specs=(VMEM,) * QUAD,
            compiler_params=params(8),
        )(*blocks, *behind)
        later.append(quad_swap(sums))

    slots = [near((rows, QUAD * count * HEAD), jnp.float32) for _, count in parts]
    grad_query, *local = pl.pallas_call(
        functools.partial(local_kernel, each, parts),
        out_shape=(half, *slots, *slots),
        in_specs=[VMEM] * (5 + len(grads)),
        out_specs=(VMEM,) * (1 + 2 * len(parts)),
        compiler_params=params(8),
    )(q, k, v, s, probs, *grads)
    done = ()
    for part, (start, count) in enumerate(parts):
        stage = pltpu.VMEM((rows, QUAD * count * HEAD), jnp.bfloat16)
        done = pl.pallas_call(
            functools.partial(final_kernel, each, start, count),
            out_shape=(half, half),
            in_specs=[VMEM] * (4 + QUAD) + [HBM] * len(done),
            out_specs=(HBM,) * 2,
            scratch_shapes=[stage, stage, pltpu.SemaphoreType.DMA((QUAD, 2))],
            input_output_aliases={4 + QUAD + index: index for index in range(len(done))},
            compiler_params=params(8),
        )(k, v, local[part], local[len(parts) + part], *later[part], *done)
    return (grad_query, *done)


def solution(mesh):
    rows = P(("groups", "ctx"), "tp")
    return jax.shard_map(
        per_device,
        mesh=mesh,
        in_specs=(rows, rows, rows, rows, P(("groups", "ctx"), "tp", None, None), P("tp")),
        out_specs=(rows, rows, rows),
        check_vma=False,
    )
```

```python
import functools

import jax
import jax.numpy as jnp
from jax import lax
from jax.experimental import pallas as pl
from jax.experimental.pallas import tpu as pltpu
from jax.sharding import PartitionSpec as P

HEAD = 128
QUAD = 4
SPLIT = (2, 2)
STEPS = (2, 1, 3, 0)
CALLS = (
    (((0, 2),), None),
    (((0, 1), (0, 3), (0, 0)), None),
    (((1, 2), (1, 1), (1, 3), (1, 0)), (0, 2)),
)
VMEM = pl.BlockSpec(memory_space=pltpu.VMEM)
ANY = pl.BlockSpec(memory_space=pl.ANY)
HBM = pl.BlockSpec(memory_space=pltpu.HBM)
NN = (((1,), (0,)), ((), ()))
NT = (((1,), (1,)), ((), ()))
TN = (((0,), (0,)), ((), ()))


def dot(left, right, dims):
    return lax.dot_general(left, right, dims, preferred_element_type=jnp.float32)


def columns(head, count=1):
    if isinstance(head, int):
        return pl.ds(head * HEAD, count * HEAD)
    return pl.ds(pl.multiple_of(head * HEAD, HEAD), count * HEAD)


def turn(step):
    core = lax.rem(lax.axis_index("tp"), 2)
    return {0: 0, 1: 1 + core, 2: 2 - core, 3: 3}[step]


def lower(rows):
    row = lax.broadcasted_iota(jnp.int32, (rows, rows), 0)
    return row >= lax.broadcasted_iota(jnp.int32, (rows, rows), 1)


def parts_of(heads):
    each = heads // QUAD
    parts, start = [], 0
    for index, count in enumerate(SPLIT):
        count = each - start if index == len(SPLIT) - 1 else count
        parts.append((start, count))
        start += count
    return each, parts


def forward_kernel(
    q_hbm, k_hbm, v_hbm, s_hbm, y_hbm, gain_hbm,
    out_ref, probs_ref, stat_ref, q_ref, k_ref, v_ref, s_ref, y_ref, gain_ref, sems,
):
    rows, width = q_ref.shape
    pairs = ((q_hbm, q_ref), (k_hbm, k_ref), (v_hbm, v_ref), (s_hbm, s_ref), (gain_hbm, gain_ref))
    pairs += ((y_hbm, y_ref),)
    copies = [
        pltpu.make_async_copy(source, target, sems.at[index])
        for index, (source, target) in enumerate(pairs)
    ]
    for copy in copies:
        copy.start()
    mask = lower(rows)
    heads = [(head, columns(head)) for head in range(width // HEAD)]
    for copy in copies[:2]:
        copy.wait()
    for head, at in heads:
        scores = dot(q_ref[:, at], k_ref[:, at], NT)
        probs_ref[:, at] = jnp.where(mask, scores, 0.0).astype(jnp.bfloat16)
    for copy in copies[2:]:
        copy.wait()
    squares = jnp.zeros((rows, HEAD), jnp.float32)
    crosses = jnp.zeros((rows, HEAD), jnp.float32)
    for head, at in heads:
        out = dot(probs_ref[:, at], v_ref[:, at], NN) + dot(q_ref[:, at], s_ref[head], NN)
        out_ref[:, at] = out
        squares += out * out
        crosses += gain_ref[:, at] * y_ref[:, at].astype(jnp.float32) * out
    lane = lax.broadcasted_iota(jnp.int32, (rows, HEAD), 1)
    square = jnp.sum(squares, axis=1, keepdims=True)
    cross = jnp.sum(crosses, axis=1, keepdims=True)
    stat_ref[...] = jnp.where(lane == 0, square, cross)


def state_kernel(features, each, parts, pieces, own_ref, other_ref, out_ref, y_ref, gain_ref, q_ref, *refs):
    g_ref, *u_refs = refs[-1 - len(pieces) :]
    stat = own_ref[...] + other_ref[...]
    square, cross = stat[:, 0:1], stat[:, 1:2]
    inverse = lax.rsqrt(square / features + 1e-06)
    back = cross * (inverse * inverse * inverse) / features
    me = lax.rem(lax.axis_index("ctx"), QUAD)
    slot = 0
    for (part, step), u_ref in zip(pieces, u_refs):
        start, count = parts[part]
        for local in range(count):
            at = columns((me ^ step) * each + start + local)
            weighted = gain_ref[:, at] * y_ref[:, at].astype(jnp.float32)
            grad = (inverse * weighted - out_ref[:, at] * back).astype(jnp.bfloat16)
            g_ref[:, columns(slot)] = grad
            slot += 1
            u_ref[local] = dot(q_ref[:, at], grad, TN)


def suffix_kernel(*refs):
    block_refs, behind_refs, sum_refs = refs[:QUAD], refs[QUAD:-QUAD], refs[-QUAD:]
    place = lax.axis_index("ctx")
    me = lax.rem(place, QUAD)
    blocks = [ref[...] for ref in block_refs]
    behind = jnp.zeros_like(blocks[0])
    for level, ref in enumerate(behind_refs):
        behind += jnp.where((place & (QUAD << level)) == 0, ref[...], 0.0)
    for target, step in enumerate(STEPS):
        value = behind
        for source, other in enumerate(STEPS):
            value += jnp.where((me ^ other) > (me ^ turn(step)), blocks[source], 0.0)
        sum_refs[target][...] = value


def local_kernel(each, parts, q_ref, k_ref, v_ref, s_ref, probs_ref, *refs):
    g_refs, query_ref = refs[: len(CALLS)], refs[len(CALLS)]
    key_refs = refs[len(CALLS) + 1 : len(CALLS) + 1 + len(parts)]
    value_refs = refs[len(CALLS) + 1 + len(parts) :]
    mask = lower(q_ref.shape[0])
    me = lax.rem(lax.axis_index("ctx"), QUAD)
    for (pieces, _), g_ref in zip(CALLS, g_refs):
        place = 0
        for part, step in pieces:
            start, count = parts[part]
            for local in range(count):
                head = (me ^ step) * each + start + local
                at, slot = columns(head), columns(STEPS.index(step) * count + local)
                g = g_ref[:, columns(place)]
                place += 1
                grads = jnp.where(mask, dot(g, v_ref[:, at], NT), 0.0).astype(jnp.bfloat16)
                query = dot(grads, k_ref[:, at], NN) + dot(g, s_ref[head], NT)
                query_ref[:, at] = query.astype(jnp.bfloat16)
                key_refs[part][:, slot] = dot(grads, q_ref[:, at], TN)
                value_refs[part][:, slot] = dot(probs_ref[:, at], g, TN)


def final_kernel(each, start, count, k_ref, v_ref, key_in, value_in, *refs):
    later_refs = refs[:QUAD]
    key_hbm, value_hbm, key_ref, value_ref, sems = refs[-5:]
    me = lax.rem(lax.axis_index("ctx"), QUAD)
    copies = []
    for index, step in enumerate(STEPS):
        slots = columns(index * count, count)
        for local in range(count):
            at = columns((me ^ turn(step)) * each + start + local)
            slot = columns(index * count + local)
            held = index if index > 1 else lax.rem(lax.axis_index("tp") + index, 2)
            source = columns(held * count + local)
            later = later_refs[index][local].astype(jnp.bfloat16)
            key = key_in[:, source] + dot(v_ref[:, at], later, NT)
            key_ref[:, slot] = key.astype(jnp.bfloat16)
            value = value_in[:, source] + dot(k_ref[:, at], later, NN)
            value_ref[:, slot] = value.astype(jnp.bfloat16)
        at = columns((me ^ turn(step)) * each + start, count)
        for pair, (source, target) in enumerate(((key_ref, key_hbm), (value_ref, value_hbm))):
            copy = pltpu.make_async_copy(source.at[:, slots], target.at[:, at], sems.at[index, pair])
            copy.start()
            copies.append(copy)
    for copy in copies:
        copy.wait()


def params(mib):
    return pltpu.CompilerParams(vmem_limit_bytes=mib << 20)


def partner(value, axis, mask):
    count = lax.axis_size(axis)
    return lax.ppermute(value, axis, [(source, source ^ mask) for source in range(count)])


def quad_swap(pieces):
    return [
        partner(piece, "ctx", step) if step else piece for piece, step in zip(pieces, STEPS)
    ]


def return_swap(pieces):
    cores = lax.axis_size("tp")
    places = range(lax.axis_size("ctx"))
    came = []
    for piece, step in zip(pieces, STEPS):
        pairs = []
        for place in places:
            for core in range(cores):
                other = {0: 0, 1: 1 + core % 2, 2: 2 - core % 2, 3: 3}[step]
                pairs.append((place * cores + core, (place ^ other) * cores + core))
        came.append(lax.ppermute(piece, ("ctx", "tp"), pairs) if step else piece)
    return came


def per_device(queries, keys, values, grad_y, state_low, gain):
    rows, width = queries.shape
    heads = width // HEAD
    each, parts = parts_of(heads)
    features = width * lax.axis_size("tp")
    state = state_low[0]
    gain_row = gain.reshape(1, width)

    near = pltpu.VMEM
    half = jax.ShapeDtypeStruct((rows, width), jnp.bfloat16)
    held_half = near((rows, width), jnp.bfloat16)
    operands = (queries, keys, values, state, grad_y, gain_row)
    out, probs, stat, q, k, v, s, y, gain_v = pl.pallas_call(
        forward_kernel,
        out_shape=(
            near((rows, width), jnp.float32),
            held_half,
            near((rows, HEAD), jnp.float32),
            held_half,
            held_half,
            held_half,
            near(state.shape, state.dtype),
            held_half,
            near(gain_row.shape, gain_row.dtype),
        ),
        in_specs=[HBM] * 6,
        out_specs=(VMEM,) * 9,
        scratch_shapes=[pltpu.SemaphoreType.DMA((6,))],
        compiler_params=params(8),
    )(*(pltpu.with_memory_space_constraint(value, pltpu.HBM) for value in operands))
    other = partner(stat, "tp", 1)

    grads, found = [], {}
    for pieces, token in CALLS:
        tokens = [found[token]] if token else []
        shapes = [near((parts[part][1], HEAD, HEAD), jnp.float32) for part, _ in pieces]
        wide = sum(shape.shape[0] for shape in shapes) * HEAD
        grad, *own = pl.pallas_call(
            functools.partial(state_kernel, features, each, parts, pieces),
            out_shape=(near((rows, wide), jnp.bfloat16), *shapes),
            in_specs=[VMEM] * 6 + [ANY] * len(tokens),
            out_specs=(VMEM,) * (1 + len(pieces)),
            compiler_params=params(8),
        )(stat, other, out, y, gain_v, q, *tokens)
        grads.append(grad)
        for (part, step), piece in zip(pieces, own):
            found[part, step] = partner(piece, "ctx", step) if step else piece
    held = [[found[part, step] for step in STEPS] for part in range(len(parts))]
    later = []
    for blocks in held:
        total = blocks[0] + blocks[1] + blocks[2] + blocks[3]
        behind = []
        span = QUAD
        while span < lax.axis_size("ctx"):
            behind.append(partner(total, "ctx", span))
            span *= 2
            if span < lax.axis_size("ctx"):
                total = total + behind[-1]
        piece = near(total.shape, jnp.float32)
        sums = pl.pallas_call(
            suffix_kernel,
            out_shape=(piece,) * QUAD,
            in_specs=[VMEM] * (QUAD + len(behind)),
            out_specs=(VMEM,) * QUAD,
            compiler_params=params(8),
        )(*blocks, *behind)
        later.append(return_swap(sums))

    slots = [near((rows, QUAD * count * HEAD), jnp.float32) for _, count in parts]
    grad_query, *local = pl.pallas_call(
        functools.partial(local_kernel, each, parts),
        out_shape=(half, *slots, *slots),
        in_specs=[VMEM] * (5 + len(grads)),
        out_specs=(VMEM,) * (1 + 2 * len(parts)),
        compiler_params=params(8),
    )(q, k, v, s, probs, *grads)
    done = ()
    for part, (start, count) in enumerate(parts):
        stage = pltpu.VMEM((rows, QUAD * count * HEAD), jnp.bfloat16)
        done = pl.pallas_call(
            functools.partial(final_kernel, each, start, count),
            out_shape=(half, half),
            in_specs=[VMEM] * (4 + QUAD) + [HBM] * len(done),
            out_specs=(HBM,) * 2,
            scratch_shapes=[stage, stage, pltpu.SemaphoreType.DMA((QUAD, 2))],
            input_output_aliases={4 + QUAD + index: index for index in range(len(done))},
            compiler_params=params(8),
        )(k, v, local[part], local[len(parts) + part], *later[part], *done)
    return (grad_query, *done)


def solution(mesh):
    rows = P(("groups", "ctx"), "tp")
    return jax.shard_map(
        per_device,
        mesh=mesh,
        in_specs=(rows, rows, rows, rows, P(("groups", "ctx"), "tp", None, None), P("tp")),
        out_specs=(rows, rows, rows),
        check_vma=False,
    )
```

```python
import functools

import jax
import jax.numpy as jnp
from jax import lax
from jax.experimental import pallas as pl
from jax.experimental.pallas import tpu as pltpu
from jax.sharding import PartitionSpec as P

HEAD = 128
QUAD = 4
SPLIT = (2, 2)
STEPS = (2, 1, 3, 0)
CALLS = (
    (((0, 2),), None),
    (((0, 1), (0, 3), (0, 0)), None),
    (((1, 2),), (0, 2)),
    (((1, 1), (1, 3), (1, 0)), (0, 2)),
)
VMEM = pl.BlockSpec(memory_space=pltpu.VMEM)
ANY = pl.BlockSpec(memory_space=pl.ANY)
HBM = pl.BlockSpec(memory_space=pltpu.HBM)
NN = (((1,), (0,)), ((), ()))
NT = (((1,), (1,)), ((), ()))
TN = (((0,), (0,)), ((), ()))


def dot(left, right, dims):
    return lax.dot_general(left, right, dims, preferred_element_type=jnp.float32)


def columns(head, count=1):
    if isinstance(head, int):
        return pl.ds(head * HEAD, count * HEAD)
    return pl.ds(pl.multiple_of(head * HEAD, HEAD), count * HEAD)


def turn(step):
    core = lax.rem(lax.axis_index("tp"), 2)
    return {0: 0, 1: 1 + core, 2: 2 - core, 3: 3}[step]


def lower(rows):
    row = lax.broadcasted_iota(jnp.int32, (rows, rows), 0)
    return row >= lax.broadcasted_iota(jnp.int32, (rows, rows), 1)


def parts_of(heads):
    each = heads // QUAD
    parts, start = [], 0
    for index, count in enumerate(SPLIT):
        count = each - start if index == len(SPLIT) - 1 else count
        parts.append((start, count))
        start += count
    return each, parts


def forward_kernel(
    q_hbm, k_hbm, v_hbm, s_hbm, y_hbm, gain_hbm,
    out_ref, probs_ref, stat_ref, q_ref, k_ref, v_ref, s_ref, y_ref, gain_ref, sems,
):
    rows, width = q_ref.shape
    pairs = ((q_hbm, q_ref), (k_hbm, k_ref), (v_hbm, v_ref), (s_hbm, s_ref), (gain_hbm, gain_ref))
    pairs += ((y_hbm, y_ref),)
    copies = [
        pltpu.make_async_copy(source, target, sems.at[index])
        for index, (source, target) in enumerate(pairs)
    ]
    for copy in copies:
        copy.start()
    mask = lower(rows)
    heads = [(head, columns(head)) for head in range(width // HEAD)]
    for copy in copies[:2]:
        copy.wait()
    for head, at in heads:
        scores = dot(q_ref[:, at], k_ref[:, at], NT)
        probs_ref[:, at] = jnp.where(mask, scores, 0.0).astype(jnp.bfloat16)
    for copy in copies[2:]:
        copy.wait()
    squares = jnp.zeros((rows, HEAD), jnp.float32)
    crosses = jnp.zeros((rows, HEAD), jnp.float32)
    for head, at in heads:
        out = dot(probs_ref[:, at], v_ref[:, at], NN) + dot(q_ref[:, at], s_ref[head], NN)
        out_ref[:, at] = out
        squares += out * out
        crosses += gain_ref[:, at] * y_ref[:, at].astype(jnp.float32) * out
    lane = lax.broadcasted_iota(jnp.int32, (rows, HEAD), 1)
    square = jnp.sum(squares, axis=1, keepdims=True)
    cross = jnp.sum(crosses, axis=1, keepdims=True)
    stat_ref[...] = jnp.where(lane == 0, square, cross)


def state_kernel(features, each, parts, pieces, own_ref, other_ref, out_ref, y_ref, gain_ref, q_ref, *refs):
    g_ref, *u_refs = refs[-1 - len(pieces) :]
    stat = own_ref[...] + other_ref[...]
    square, cross = stat[:, 0:1], stat[:, 1:2]
    inverse = lax.rsqrt(square / features + 1e-06)
    back = cross * (inverse * inverse * inverse) / features
    me = lax.rem(lax.axis_index("ctx"), QUAD)
    slot = 0
    for (part, step), u_ref in zip(pieces, u_refs):
        start, count = parts[part]
        for local in range(count):
            at = columns((me ^ step) * each + start + local)
            weighted = gain_ref[:, at] * y_ref[:, at].astype(jnp.float32)
            grad = (inverse * weighted - out_ref[:, at] * back).astype(jnp.bfloat16)
            g_ref[:, columns(slot)] = grad
            slot += 1
            u_ref[local] = dot(q_ref[:, at], grad, TN)


def suffix_kernel(*refs):
    block_refs, behind_refs, sum_refs = refs[:QUAD], refs[QUAD:-QUAD], refs[-QUAD:]
    place = lax.axis_index("ctx")
    me = lax.rem(place, QUAD)
    blocks = [ref[...] for ref in block_refs]
    behind = jnp.zeros_like(blocks[0])
    for level, ref in enumerate(behind_refs):
        behind += jnp.where((place & (QUAD << level)) == 0, ref[...], 0.0)
    for target, step in enumerate(STEPS):
        value = behind
        for source, other in enumerate(STEPS):
            value += jnp.where((me ^ other) > (me ^ turn(step)), blocks[source], 0.0)
        sum_refs[target][...] = value


def local_kernel(each, parts, q_ref, k_ref, v_ref, s_ref, probs_ref, *refs):
    g_refs, query_ref = refs[: len(CALLS)], refs[len(CALLS)]
    key_refs = refs[len(CALLS) + 1 : len(CALLS) + 1 + len(parts)]
    value_refs = refs[len(CALLS) + 1 + len(parts) :]
    mask = lower(q_ref.shape[0])
    me = lax.rem(lax.axis_index("ctx"), QUAD)
    for (pieces, _), g_ref in zip(CALLS, g_refs):
        place = 0
        for part, step in pieces:
            start, count = parts[part]
            for local in range(count):
                head = (me ^ step) * each + start + local
                at, slot = columns(head), columns(STEPS.index(step) * count + local)
                g = g_ref[:, columns(place)]
                place += 1
                grads = jnp.where(mask, dot(g, v_ref[:, at], NT), 0.0).astype(jnp.bfloat16)
                query = dot(grads, k_ref[:, at], NN) + dot(g, s_ref[head], NT)
                query_ref[:, at] = query.astype(jnp.bfloat16)
                key_refs[part][:, slot] = dot(grads, q_ref[:, at], TN)
                value_refs[part][:, slot] = dot(probs_ref[:, at], g, TN)


def final_kernel(each, start, count, k_ref, v_ref, key_in, value_in, *refs):
    later_refs = refs[:QUAD]
    key_hbm, value_hbm, key_ref, value_ref, sems = refs[-5:]
    me = lax.rem(lax.axis_index("ctx"), QUAD)
    copies = []
    for index, step in enumerate(STEPS):
        slots = columns(index * count, count)
        for local in range(count):
            at = columns((me ^ turn(step)) * each + start + local)
            slot = columns(index * count + local)
            held = index if index > 1 else lax.rem(lax.axis_index("tp") + index, 2)
            source = columns(held * count + local)
            later = later_refs[index][local].astype(jnp.bfloat16)
            key = key_in[:, source] + dot(v_ref[:, at], later, NT)
            key_ref[:, slot] = key.astype(jnp.bfloat16)
            value = value_in[:, source] + dot(k_ref[:, at], later, NN)
            value_ref[:, slot] = value.astype(jnp.bfloat16)
        at = columns((me ^ turn(step)) * each + start, count)
        for pair, (source, target) in enumerate(((key_ref, key_hbm), (value_ref, value_hbm))):
            copy = pltpu.make_async_copy(source.at[:, slots], target.at[:, at], sems.at[index, pair])
            copy.start()
            copies.append(copy)
    for copy in copies:
        copy.wait()


def params(mib):
    return pltpu.CompilerParams(vmem_limit_bytes=mib << 20)


def partner(value, axis, mask):
    count = lax.axis_size(axis)
    return lax.ppermute(value, axis, [(source, source ^ mask) for source in range(count)])


def quad_swap(pieces):
    return [
        partner(piece, "ctx", step) if step else piece for piece, step in zip(pieces, STEPS)
    ]


def return_swap(pieces):
    cores = lax.axis_size("tp")
    places = range(lax.axis_size("ctx"))
    came = []
    for piece, step in zip(pieces, STEPS):
        pairs = []
        for place in places:
            for core in range(cores):
                other = {0: 0, 1: 1 + core % 2, 2: 2 - core % 2, 3: 3}[step]
                pairs.append((place * cores + core, (place ^ other) * cores + core))
        came.append(lax.ppermute(piece, ("ctx", "tp"), pairs) if step else piece)
    return came


def per_device(queries, keys, values, grad_y, state_low, gain):
    rows, width = queries.shape
    heads = width // HEAD
    each, parts = parts_of(heads)
    features = width * lax.axis_size("tp")
    state = state_low[0]
    gain_row = gain.reshape(1, width)

    near = pltpu.VMEM
    half = jax.ShapeDtypeStruct((rows, width), jnp.bfloat16)
    held_half = near((rows, width), jnp.bfloat16)
    operands = (queries, keys, values, state, grad_y, gain_row)
    out, probs, stat, q, k, v, s, y, gain_v = pl.pallas_call(
        forward_kernel,
        out_shape=(
            near((rows, width), jnp.float32),
            held_half,
            near((rows, HEAD), jnp.float32),
            held_half,
            held_half,
            held_half,
            near(state.shape, state.dtype),
            held_half,
            near(gain_row.shape, gain_row.dtype),
        ),
        in_specs=[HBM] * 6,
        out_specs=(VMEM,) * 9,
        scratch_shapes=[pltpu.SemaphoreType.DMA((6,))],
        compiler_params=params(8),
    )(*(pltpu.with_memory_space_constraint(value, pltpu.HBM) for value in operands))
    other = partner(stat, "tp", 1)

    grads, found = [], {}
    for pieces, token in CALLS:
        tokens = [found[token]] if token else []
        shapes = [near((parts[part][1], HEAD, HEAD), jnp.float32) for part, _ in pieces]
        wide = sum(shape.shape[0] for shape in shapes) * HEAD
        grad, *own = pl.pallas_call(
            functools.partial(state_kernel, features, each, parts, pieces),
            out_shape=(near((rows, wide), jnp.bfloat16), *shapes),
            in_specs=[VMEM] * 6 + [ANY] * len(tokens),
            out_specs=(VMEM,) * (1 + len(pieces)),
            compiler_params=params(8),
        )(stat, other, out, y, gain_v, q, *tokens)
        grads.append(grad)
        for (part, step), piece in zip(pieces, own):
            found[part, step] = partner(piece, "ctx", step) if step else piece
    held = [[found[part, step] for step in STEPS] for part in range(len(parts))]
    later = []
    for blocks in held:
        total = blocks[0] + blocks[1] + blocks[2] + blocks[3]
        behind = []
        span = QUAD
        while span < lax.axis_size("ctx"):
            behind.append(partner(total, "ctx", span))
            span *= 2
            if span < lax.axis_size("ctx"):
                total = total + behind[-1]
        piece = near(total.shape, jnp.float32)
        sums = pl.pallas_call(
            suffix_kernel,
            out_shape=(piece,) * QUAD,
            in_specs=[VMEM] * (QUAD + len(behind)),
            out_specs=(VMEM,) * QUAD,
            compiler_params=params(8),
        )(*blocks, *behind)
        later.append(return_swap(sums))

    slots = [near((rows, QUAD * count * HEAD), jnp.float32) for _, count in parts]
    grad_query, *local = pl.pallas_call(
        functools.partial(local_kernel, each, parts),
        out_shape=(half, *slots, *slots),
        in_specs=[VMEM] * (5 + len(grads)),
        out_specs=(VMEM,) * (1 + 2 * len(parts)),
        compiler_params=params(8),
    )(q, k, v, s, probs, *grads)
    done = ()
    for part, (start, count) in enumerate(parts):
        stage = pltpu.VMEM((rows, QUAD * count * HEAD), jnp.bfloat16)
        done = pl.pallas_call(
            functools.partial(final_kernel, each, start, count),
            out_shape=(half, half),
            in_specs=[VMEM] * (4 + QUAD) + [HBM] * len(done),
            out_specs=(HBM,) * 2,
            scratch_shapes=[stage, stage, pltpu.SemaphoreType.DMA((QUAD, 2))],
            input_output_aliases={4 + QUAD + index: index for index in range(len(done))},
            compiler_params=params(8),
        )(k, v, local[part], local[len(parts) + part], *later[part], *done)
    return (grad_query, *done)


def solution(mesh):
    rows = P(("groups", "ctx"), "tp")
    return jax.shard_map(
        per_device,
        mesh=mesh,
        in_specs=(rows, rows, rows, rows, P(("groups", "ctx"), "tp", None, None), P("tp")),
        out_specs=(rows, rows, rows),
        check_vma=False,
    )
```

```python
import functools

import jax
import jax.numpy as jnp
from jax import lax
from jax.experimental import pallas as pl
from jax.experimental.pallas import tpu as pltpu
from jax.sharding import PartitionSpec as P

HEAD = 128
QUAD = 4
SPLIT = (2, 2)
STEPS = (2, 1, 3, 0)
CALLS = (
    (((0, 2),), None),
    (((0, 1), (0, 3), (0, 0)), None),
    (((1, 2), (1, 1), (1, 3), (1, 0)), (0, 2)),
)
VMEM = pl.BlockSpec(memory_space=pltpu.VMEM)
ANY = pl.BlockSpec(memory_space=pl.ANY)
HBM = pl.BlockSpec(memory_space=pltpu.HBM)
NN = (((1,), (0,)), ((), ()))
NT = (((1,), (1,)), ((), ()))
TN = (((0,), (0,)), ((), ()))


def dot(left, right, dims):
    return lax.dot_general(left, right, dims, preferred_element_type=jnp.float32)


def columns(head, count=1):
    if isinstance(head, int):
        return pl.ds(head * HEAD, count * HEAD)
    return pl.ds(pl.multiple_of(head * HEAD, HEAD), count * HEAD)


def turn(step):
    core = lax.rem(lax.axis_index("tp"), 2)
    return {0: 0, 1: 1 + core, 2: 2 - core, 3: 3}[step]


def lower(rows):
    row = lax.broadcasted_iota(jnp.int32, (rows, rows), 0)
    return row >= lax.broadcasted_iota(jnp.int32, (rows, rows), 1)


def parts_of(heads):
    each = heads // QUAD
    parts, start = [], 0
    for index, count in enumerate(SPLIT):
        count = each - start if index == len(SPLIT) - 1 else count
        parts.append((start, count))
        start += count
    return each, parts


def forward_kernel(
    q_hbm, k_hbm, v_hbm, s_hbm, y_hbm, gain_hbm,
    out_ref, probs_ref, stat_ref, q_ref, k_ref, v_ref, s_ref, y_ref, gain_ref, sems,
):
    rows, width = q_ref.shape
    pairs = ((q_hbm, q_ref), (k_hbm, k_ref), (v_hbm, v_ref), (s_hbm, s_ref), (gain_hbm, gain_ref))
    pairs += ((y_hbm, y_ref),)
    copies = [
        pltpu.make_async_copy(source, target, sems.at[index])
        for index, (source, target) in enumerate(pairs)
    ]
    for copy in copies:
        copy.start()
    mask = lower(rows)
    heads = [(head, columns(head)) for head in range(width // HEAD)]
    for copy in copies[:2]:
        copy.wait()
    for head, at in heads:
        scores = dot(q_ref[:, at], k_ref[:, at], NT)
        probs_ref[:, at] = jnp.where(mask, scores, 0.0).astype(jnp.bfloat16)
    for copy in copies[2:]:
        copy.wait()
    squares = jnp.zeros((rows, HEAD), jnp.float32)
    crosses = jnp.zeros((rows, HEAD), jnp.float32)
    for head, at in heads:
        out = dot(probs_ref[:, at], v_ref[:, at], NN) + dot(q_ref[:, at], s_ref[head], NN)
        out_ref[:, at] = out
        squares += out * out
        crosses += gain_ref[:, at] * y_ref[:, at].astype(jnp.float32) * out
    lane = lax.broadcasted_iota(jnp.int32, (rows, HEAD), 1)
    square = jnp.sum(squares, axis=1, keepdims=True)
    cross = jnp.sum(crosses, axis=1, keepdims=True)
    stat_ref[...] = jnp.where(lane == 0, square, cross)


def state_kernel(features, each, parts, pieces, own_ref, other_ref, out_ref, y_ref, gain_ref, q_ref, *refs):
    g_ref, *u_refs = refs[-1 - len(pieces) :]
    stat = own_ref[...] + other_ref[...]
    square, cross = stat[:, 0:1], stat[:, 1:2]
    inverse = lax.rsqrt(square / features + 1e-06)
    back = cross * (inverse * inverse * inverse) / features
    me = lax.rem(lax.axis_index("ctx"), QUAD)
    slot = 0
    for (part, step), u_ref in zip(pieces, u_refs):
        start, count = parts[part]
        for local in range(count):
            at = columns((me ^ step) * each + start + local)
            weighted = gain_ref[:, at] * y_ref[:, at].astype(jnp.float32)
            grad = (inverse * weighted - out_ref[:, at] * back).astype(jnp.bfloat16)
            g_ref[:, columns(slot)] = grad
            slot += 1
            u_ref[local] = dot(q_ref[:, at], grad, TN)


def suffix_kernel(*refs):
    block_refs, behind_refs, sum_refs = refs[:QUAD], refs[QUAD:-QUAD], refs[-QUAD:]
    place = lax.axis_index("ctx")
    me = lax.rem(place, QUAD)
    blocks = [ref[...] for ref in block_refs]
    behind = jnp.zeros_like(blocks[0])
    for level, ref in enumerate(behind_refs):
        behind += jnp.where((place & (QUAD << level)) == 0, ref[...], 0.0)
    for target, step in enumerate(STEPS):
        value = behind
        for source, other in enumerate(STEPS):
            value += jnp.where((me ^ other) > (me ^ turn(step)), blocks[source], 0.0)
        sum_refs[target][...] = value


def local_kernel(each, parts, q_ref, k_ref, v_ref, s_ref, probs_ref, *refs):
    g_refs, query_ref = refs[: len(CALLS)], refs[len(CALLS)]
    key_refs = refs[len(CALLS) + 1 : len(CALLS) + 1 + len(parts)]
    value_refs = refs[len(CALLS) + 1 + len(parts) :]
    mask = lower(q_ref.shape[0])
    me = lax.rem(lax.axis_index("ctx"), QUAD)
    for (pieces, _), g_ref in zip(CALLS, g_refs):
        place = 0
        for part, step in pieces:
            start, count = parts[part]
            for local in range(count):
                head = (me ^ step) * each + start + local
                at, slot = columns(head), columns(STEPS.index(step) * count + local)
                g = g_ref[:, columns(place)]
                place += 1
                grads = jnp.where(mask, dot(g, v_ref[:, at], NT), 0.0).astype(jnp.bfloat16)
                query = dot(grads, k_ref[:, at], NN) + dot(g, s_ref[head], NT)
                query_ref[:, at] = query.astype(jnp.bfloat16)
                key_refs[part][:, slot] = dot(grads, q_ref[:, at], TN)
                value_refs[part][:, slot] = dot(probs_ref[:, at], g, TN)


def final_kernel(each, start, count, k_ref, v_ref, key_in, value_in, *refs):
    later_refs = refs[:QUAD]
    key_hbm, value_hbm, key_ref, value_ref, sems = refs[-5:]
    me = lax.rem(lax.axis_index("ctx"), QUAD)
    copies = []
    for index, step in enumerate(STEPS):
        slots = columns(index * count, count)
        for local in range(count):
            at = columns((me ^ turn(step)) * each + start + local)
            slot = columns(index * count + local)
            held = index if index > 1 else lax.rem(lax.axis_index("tp") + index, 2)
            source = columns(held * count + local)
            later = later_refs[index][local].astype(jnp.bfloat16)
            key = key_in[:, source] + dot(v_ref[:, at], later, NT)
            key_ref[:, slot] = key.astype(jnp.bfloat16)
            value = value_in[:, source] + dot(k_ref[:, at], later, NN)
            value_ref[:, slot] = value.astype(jnp.bfloat16)
        at = columns((me ^ turn(step)) * each + start, count)
        for pair, (source, target) in enumerate(((key_ref, key_hbm), (value_ref, value_hbm))):
            copy = pltpu.make_async_copy(source.at[:, slots], target.at[:, at], sems.at[index, pair])
            copy.start()
            copies.append(copy)
    for copy in copies:
        copy.wait()


def params(mib):
    return pltpu.CompilerParams(vmem_limit_bytes=mib << 20)


def partner(value, axis, mask):
    count = lax.axis_size(axis)
    return lax.ppermute(value, axis, [(source, source ^ mask) for source in range(count)])


def quad_swap(pieces):
    return [
        partner(piece, "ctx", step) if step else piece for piece, step in zip(pieces, STEPS)
    ]


def return_swap(pieces):
    cores = lax.axis_size("tp")
    places = range(lax.axis_size("ctx"))
    came = []
    for piece, step in zip(pieces, STEPS):
        pairs = []
        for place in places:
            for core in range(cores):
                other = {0: 0, 1: 1 + core % 2, 2: 2 - core % 2, 3: 3}[step]
                pairs.append((place * cores + core, (place ^ other) * cores + core))
        came.append(lax.ppermute(piece, ("ctx", "tp"), pairs) if step else piece)
    return came


def per_device(queries, keys, values, grad_y, state_low, gain):
    rows, width = queries.shape
    heads = width // HEAD
    each, parts = parts_of(heads)
    features = width * lax.axis_size("tp")
    state = state_low[0]
    gain_row = gain.reshape(1, width)

    near = pltpu.VMEM
    half = jax.ShapeDtypeStruct((rows, width), jnp.bfloat16)
    held_half = near((rows, width), jnp.bfloat16)
    operands = (queries, keys, values, state, grad_y, gain_row)
    out, probs, stat, q, k, v, s, y, gain_v = pl.pallas_call(
        forward_kernel,
        out_shape=(
            near((rows, width), jnp.float32),
            held_half,
            near((rows, HEAD), jnp.float32),
            held_half,
            held_half,
            held_half,
            near(state.shape, state.dtype),
            held_half,
            near(gain_row.shape, gain_row.dtype),
        ),
        in_specs=[HBM] * 6,
        out_specs=(VMEM,) * 9,
        scratch_shapes=[pltpu.SemaphoreType.DMA((6,))],
        compiler_params=params(8),
    )(*(pltpu.with_memory_space_constraint(value, pltpu.HBM) for value in operands))
    other = partner(stat, "tp", 1)

    grads, found = [], {}
    for pieces, token in CALLS:
        shapes = [near((parts[part][1], HEAD, HEAD), jnp.float32) for part, _ in pieces]
        wide = sum(shape.shape[0] for shape in shapes) * HEAD
        grad, *own = pl.pallas_call(
            functools.partial(state_kernel, features, each, parts, pieces),
            out_shape=(near((rows, wide), jnp.bfloat16), *shapes),
            in_specs=[VMEM] * 6,
            out_specs=(VMEM,) * (1 + len(pieces)),
            compiler_params=params(8),
        )(stat, other, out, y, gain_v, q)
        if token:
            own, found[token] = lax.optimization_barrier((own, found[token]))
        grads.append(grad)
        for (part, step), piece in zip(pieces, own):
            found[part, step] = partner(piece, "ctx", step) if step else piece
    held = [[found[part, step] for step in STEPS] for part in range(len(parts))]
    later = []
    for blocks in held:
        total = blocks[0] + blocks[1] + blocks[2] + blocks[3]
        behind = []
        span = QUAD
        while span < lax.axis_size("ctx"):
            behind.append(partner(total, "ctx", span))
            span *= 2
            if span < lax.axis_size("ctx"):
                total = total + behind[-1]
        piece = near(total.shape, jnp.float32)
        sums = pl.pallas_call(
            suffix_kernel,
            out_shape=(piece,) * QUAD,
            in_specs=[VMEM] * (QUAD + len(behind)),
            out_specs=(VMEM,) * QUAD,
            compiler_params=params(8),
        )(*blocks, *behind)
        later.append(return_swap(sums))

    slots = [near((rows, QUAD * count * HEAD), jnp.float32) for _, count in parts]
    grad_query, *local = pl.pallas_call(
        functools.partial(local_kernel, each, parts),
        out_shape=(half, *slots, *slots),
        in_specs=[VMEM] * (5 + len(grads)),
        out_specs=(VMEM,) * (1 + 2 * len(parts)),
        compiler_params=params(8),
    )(q, k, v, s, probs, *grads)
    done = ()
    for part, (start, count) in enumerate(parts):
        stage = pltpu.VMEM((rows, QUAD * count * HEAD), jnp.bfloat16)
        done = pl.pallas_call(
            functools.partial(final_kernel, each, start, count),
            out_shape=(half, half),
            in_specs=[VMEM] * (4 + QUAD) + [HBM] * len(done),
            out_specs=(HBM,) * 2,
            scratch_shapes=[stage, stage, pltpu.SemaphoreType.DMA((QUAD, 2))],
            input_output_aliases={4 + QUAD + index: index for index in range(len(done))},
            compiler_params=params(8),
        )(k, v, local[part], local[len(parts) + part], *later[part], *done)
    return (grad_query, *done)


def solution(mesh):
    rows = P(("groups", "ctx"), "tp")
    return jax.shard_map(
        per_device,
        mesh=mesh,
        in_specs=(rows, rows, rows, rows, P(("groups", "ctx"), "tp", None, None), P("tp")),
        out_specs=(rows, rows, rows),
        check_vma=False,
    )
```
